128 devices in a mesh: row: 16 (over x, y), col: 8 (over z, core).
Axes of the slice: x: 4, y: 4, z: 4, core: 2. Of those that a mesh axis runs over, the one named last changes fastest.
Arguments:
- eigenvectors: float32 [98304, 2048], P('row', 'col'), may hold values from -6 to 6
- reflectors: float32 [98304, 512], P('row', 'col'), may hold values from -0.01953125 to 0.01953125
- triangles: float32 [16, 32, 32], replicated, as said below
Outputs:
- transformed: float32 [98304, 2048], P('row', 'col')
The draws below stay inside these ranges and needn't reach their ends.
Inputs may be any that keep to these rules, and one draw needn't show every extreme that they name: Each triangles[k] is upper triangular with diagonal entries between 1.5 and 2.
All inputs are finite; a program needn't handle non-finite values.
Results may differ from the reference program's by a relative error of at most 0.0001.
Values sent between devices are 32-bit elements; how exact they have to be, the bound alone decides.
A program may use at most 128 MiB of HBM per device.

```python
import jax
import jax.numpy as jnp
from jax import lax

N = 98304
NB = 32
PANELS = 16
M = 2048


def draw_triangles(key, part):
    first_key, second_key = jax.random.split(key)
    diagonal = jax.random.uniform(first_key, (PANELS, NB), jnp.float32, 1.5, 2.0)
    spread = 0.15 * jax.random.normal(second_key, (PANELS, NB, NB), jnp.float32)
    upper_part = jnp.triu(spread, 1)
    identity = jnp.eye(NB, dtype=jnp.float32)
    return upper_part + identity[None, :, :] * diagonal[:, :, None]


def shard_levels(stream_key, extent, shards, least, largest):
    level = 1.0
    for dim, shards_of in shards:
        draws = jax.random.uniform(jax.random.fold_in(jax.random.fold_in(stream_key, 6), dim), (shards_of,), jnp.float32, least / len(shards), largest / len(shards))
        level = level * jnp.repeat(jnp.exp(draws), extent[dim] // shards_of).reshape((-1,) + (1,) * (len(extent) - 1 - dim))
    return level


def gaussian(rng, extent, deviation, most, cuts=(), kind=jnp.bfloat16):
    entries = jax.random.normal(rng, extent, jnp.float32) * deviation
    if len(cuts) > 0:
        entries = shard_levels(rng, extent, cuts, -0.22, 0.18) * entries
    return jnp.clip(entries, min=-most, max=most).astype(kind)


def setup_inputs(seed: int = 0) -> dict:
    arg_keys = jax.random.split(jax.random.key(seed), 4)
    eigenvectors = gaussian(arg_keys[0], (N, M), 1.0, 6.0, ((0, 16), (1, 8)), jnp.float32)
    reflectors = gaussian(arg_keys[1], (N, PANELS * NB), N ** -0.5, 0.01953125, ((0, 16), (1, 8)), jnp.float32)
    triangles = draw_triangles(jax.random.fold_in(arg_keys[3], 71), 0)
    return {"eigenvectors": eigenvectors, "reflectors": reflectors, "triangles": triangles}


def reference(eigenvectors, reflectors, triangles):
    highest = lax.Precision.HIGHEST
    current = eigenvectors
    for panel_no in range(PANELS - 1, -1, -1):
        vectors = reflectors[:, panel_no * NB:(panel_no + 1) * NB]
        products = jnp.einsum("rk,rc->kc", vectors, current, precision=highest)
        scaled = jnp.dot(triangles[panel_no], products, precision=highest)
        current = current - jnp.dot(vectors, scaled, precision=highest)
    return current
```

```python
import jax
import jax.numpy as jnp
from jax import lax
from jax.sharding import PartitionSpec as P

HIGH = lax.Precision.HIGH
HIGHEST = lax.Precision.HIGHEST


def on_device(eigenvectors, reflectors, triangles):
    panels, width = triangles.shape[0], triangles.shape[1]
    everyone = lax.all_gather(reflectors, "col", axis=1, tiled=True)
    products = jnp.einsum("rk,rc->kc", everyone, eigenvectors, precision=HIGH)
    gram = jnp.einsum("rk,rc->kc", reflectors, everyone, precision=HIGH)
    products, gram = lax.psum((products, gram), "row")
    gram = lax.all_gather(gram, "col", axis=0, tiled=True)
    scaled = [None] * panels
    rest = products
    for k in range(panels - 1, -1, -1):
        now = jnp.dot(triangles[k], rest[k * width:], precision=HIGHEST)
        scaled[k] = now
        if k:
            rest = rest[:k * width] - jnp.dot(
                gram[:k * width, k * width:(k + 1) * width], now, precision=HIGHEST)
    return eigenvectors - jnp.dot(everyone, jnp.concatenate(scaled, 0), precision=HIGH)


def solution(mesh):
    return jax.shard_map(
        on_device,
        mesh=mesh,
        in_specs=(P("row", "col"), P("row", "col"), P()),
        out_specs=P("row", "col"),
        check_vma=False,
    )
```

```python
import functools

import jax
import jax.numpy as jnp
from jax import lax
from jax.experimental import pallas as pl
from jax.experimental.pallas import tpu as pltpu
from jax.sharding import PartitionSpec as P

MESH = pl.DeviceIdType.MESH
HIGHEST = lax.Precision.HIGHEST
F32, BF16 = jnp.float32, jnp.bfloat16
CHUNKS = 8
OWN, UP, DOWN, FAR = range(4)
REL = (0, 1, 3, 2)
GRAM = ((OWN, UP), (UP, UP), (OWN, DOWN), (UP, DOWN), (OWN, OWN), (DOWN, DOWN),
        (UP, FAR), (FAR, FAR), (DOWN, FAR), (OWN, FAR))


def split(a):
    high = a.astype(BF16)
    return high, (a - high.astype(F32)).astype(BF16)


def dot3(a, b, dims=(((1,), (0,)), ((), ()))):
    d = functools.partial(lax.dot_general, dimension_numbers=dims, preferred_element_type=F32)
    return d(a[0], b[0]) + (d(a[0], b[1]) + d(a[1], b[0]))


NT = (((1,), (1,)), ((), ()))


def gather_kernel(rows, vt_in, x_in, t_ref, wh_ref, wl_ref, vnh_out, vnl_out,
                  vt, xb, xh, xl, vnh, vnl, pacc, pred, gacc, gh, gf, mref,
                  rs_e, rs_g, rs_l,
                  lsem, xsem, sbs, sbr, zs, zr, rss, rsr, ags, agr, gxs, gxr, osem):
    me = lax.axis_index("row")
    col = lax.axis_index("col")
    z, k = lax.div(col, 2), lax.rem(col, 2)
    up = lax.rem(z + 1, 4) * 2 + k
    down = lax.rem(z + 3, 4) * 2 + k
    sib = z * 2 + 1 - k
    lanes = vt.shape[-1]

    barrier = pltpu.get_barrier_semaphore()
    for other in (up, down, sib):
        pl.semaphore_signal(barrier, inc=1, device_id=(me, other), device_id_type=MESH)
    for d in range(1, rows):
        pl.semaphore_signal(barrier, inc=1, device_id=(lax.rem(me + d, rows), col), device_id_type=MESH)

    def own(c):
        return vt_in.at[:, pl.ds(pl.multiple_of(c * lanes, lanes), lanes)]

    def local(c):
        return pltpu.make_async_copy(own(c), vt.at[OWN, c, k], lsem.at[c])

    def load_x(c):
        return pltpu.make_async_copy(x_in.at[pl.ds(pl.multiple_of(c * lanes, lanes), lanes)], xb.at[c], xsem.at[c])

    def remote(src, dst, ssem, rsem, target):
        return pltpu.make_async_remote_copy(src_ref=src, dst_ref=dst, send_sem=ssem, recv_sem=rsem,
                                            device_id=target, device_id_type=MESH)

    def z_own(way, c):
        return remote(own(c), vt.at[(UP, DOWN)[way], c, k], zs.at[way, c], zr.at[way, c], (me, (down, up)[way]))

    def z_pass(way, j):
        c = (j, CHUNKS // 2 + j)[way]
        return remote(vt.at[(UP, DOWN)[way], c, k], vt.at[FAR, c, k],
                      zs.at[way, CHUNKS + j], zr.at[way, CHUNKS + j], (me, (down, up)[way]))

    def to_sib(slot, c):
        src = own(c) if slot == OWN else vt.at[slot, c, k]
        return remote(src, vt.at[slot, c, k], sbs.at[slot, c], sbr.at[slot, c], (me, sib))

    def peer(d):
        return lax.rem(me + d, rows)

    def rs(kind, d):
        p = peer(d)
        src = (pacc.at[pl.ds(0, 3), p], gacc.at[pl.ds(3 * p, 3)], pacc.at[pl.ds(3, 1), p])[kind]
        dst = (rs_e, rs_g, rs_l)[kind].at[d]
        return remote(src, dst, rss.at[kind, d], rsr.at[kind, d], (p, col))

    def piece(kind, owner):
        return (pred.at[pl.ds(0, 3), owner], gh.at[k, pl.ds(3 * owner, 3)], pred.at[pl.ds(3, 1), owner])[kind]

    def ag_send(kind, d):
        return remote(piece(kind, me), piece(kind, me), ags.at[kind, d], agr.at[kind, d], (peer(d), col))

    def ag_recv(kind, d):
        source = lax.rem(me + rows - d, rows)
        return remote(piece(kind, source), piece(kind, source), ags.at[kind, d], agr.at[kind, d], (peer(d), col))

    def each(fn):
        lax.fori_loop(1, rows, lambda d, _: (fn(d), 0)[1], 0)

    def reduce_scatter(kind):
        each(lambda d: rs(kind, d).start())

    def sum_and_gather(kind):
        each(lambda d: rs(kind, d).wait_recv())
        buf = (rs_e, rs_g, rs_l)[kind]
        total = (pacc[0:3, me], gacc[pl.ds(3 * me, 3)], pacc[3:4, me])[kind]
        for d in range(1, rows):
            total = total + buf[d]
        if kind == 1:
            gh[k, pl.ds(3 * me, 3)] = total
        elif kind == 0:
            pred[0:3, me] = total
        else:
            pred[3:4, me] = total
        each(lambda d: ag_send(kind, d).start())

    def finish_gather(kind):
        each(lambda d: ag_recv(kind, d).wait_recv())

    def gx(i):
        half = pl.ds(0, 48)
        if i == 0:
            return remote(gh.at[k, pl.ds(0, 16)], gh.at[k, pl.ds(48, 16)], gxs.at[0], gxr.at[0], (me, down))
        if i == 1:
            return remote(gh.at[k, pl.ds(16, 16)], gh.at[k, pl.ds(64, 16)], gxs.at[1], gxr.at[1], (me, up))
        if i == 3:
            half = pl.ds(48, 32)
        return remote(gh.at[k, half], gh.at[k, half], gxs.at[i], gxr.at[i], (me, sib))

    def store_out(c):
        return (pltpu.make_async_copy(vnh.at[c], vnh_out.at[c], osem.at[0, c]),
                pltpu.make_async_copy(vnl.at[c], vnl_out.at[c], osem.at[1, c]))

    def block(slot, c):
        return vt[slot, c].reshape(2 * vt.shape[3], lanes)

    def apply(slot, c, first):
        v = block(slot, c)
        p = dot3(split(v), (xh[c], xl[c])).reshape(16, 8, 256)
        th, tl = split(v.T)
        vnh[c, :, slot * 128:(slot + 1) * 128] = th
        vnl[c, :, slot * 128:(slot + 1) * 128] = tl
        pacc[slot] += p

    def gram(c):
        v = [split(block(s, c)) for s in (OWN, UP, DOWN)]
        a = [split(vt[s, c, k]) for s in (OWN, UP, DOWN)]
        for i, (r, s) in enumerate(GRAM[:6]):
            gacc[8 * i:8 * i + 8] += dot3(a[r], v[s], NT).reshape(8, 8, 128)

    for c in range(CHUNKS):
        local(c).start()
        load_x(c).start()
    pl.semaphore_wait(barrier, rows + 2)
    for c in range(2):
        for way in range(2):
            z_own(way, c).start()
    for c in range(CHUNKS):
        to_sib(OWN, c).start()
    pacc[...] = jnp.zeros_like(pacc)
    gacc[...] = jnp.zeros_like(gacc)

    def neighbours(c):
        to_sib(UP, c).wait_recv()
        to_sib(DOWN, c).wait_recv()
        apply(UP, c, False)
        apply(DOWN, c, False)
        gram(c)

    def step(c, _):
        load_x(c).wait()
        h, l = split(xb[c])
        xh[c] = h
        xl[c] = l
        local(c).wait()
        to_sib(OWN, c).wait_recv()
        apply(OWN, c, False)

        @pl.when(c > 0)
        def _():
            neighbours(c - 1)

        z_own(0, c).wait_recv()
        z_own(1, c).wait_recv()

        @pl.when(c < CHUNKS - 2)
        def _():
            z_own(0, c + 2).start()
            z_own(1, c + 2).start()

        @pl.when(c >= CHUNKS - 2)
        def _():
            z_pass(0, c - (CHUNKS - 2)).start()
            z_pass(1, c - (CHUNKS - 2)).start()

        to_sib(UP, c).start()
        to_sib(DOWN, c).start()
        return 0

    lax.fori_loop(0, CHUNKS, step, 0)

    def far(j):
        def one(i, _):
            c = j + i * (CHUNKS // 2)
            to_sib(FAR, c).wait_recv()
            apply(FAR, c, True)
            a, b = store_out(c)
            a.start()
            b.start()
            return 0
        lax.fori_loop(0, 2, one, 0)

    def arrived(j):
        z_pass(0, j).wait_recv()
        z_pass(1, j).wait_recv()
        if j + 2 < CHUNKS // 2:
            z_pass(0, j + 2).start()
            z_pass(1, j + 2).start()
        to_sib(FAR, j).start()
        to_sib(FAR, CHUNKS // 2 + j).start()

    neighbours(CHUNKS - 1)
    reduce_scatter(1)
    reduce_scatter(0)
    arrived(0)
    sum_and_gather(1)
    far(0)
    sum_and_gather(0)
    finish_gather(1)
    gx(0).start()
    gx(1).start()
    gx(2).start()
    arrived(1)
    far(1)
    gx(0).wait_recv()
    gx(1).wait_recv()
    gx(3).start()
    arrived(2)
    far(2)
    gx(2).wait_recv()
    gx(3).wait_recv()
    for i, (r, s) in enumerate(GRAM):
        full = gh[:, 8 * i:8 * i + 8].reshape(128, 128)
        gf[r, s] = full
        if r != s:
            gf[s, r] = full.T
    mref[...] = jnp.zeros_like(mref)
    at_row = lax.broadcasted_iota(jnp.int32, (32, 128), 0)
    at_col = lax.broadcasted_iota(jnp.int32, (32, 128), 1)
    for i in range(3, -1, -1):
        part = slice(32 * i, 32 * i + 32)
        unit = jnp.where(at_col == at_row + 32 * i, 1.0, 0.0).astype(F32)
        for slot in range(4):
            shard = lax.rem(z + REL[slot], 4)
            rest = unit - jnp.dot(gf[slot, slot, part, :], mref[slot], precision=HIGHEST)
            mref[slot, part, :] = jnp.dot(t_ref[4 * shard + i], rest, precision=HIGHEST)
    finish_gather(0)

    arrived(3)
    far(3)
    reduce_scatter(2)
    sum_and_gather(2)
    finish_gather(2)

    def slot_of(shard):
        rel = lax.rem(shard - z + 4, 4)
        return rel + lax.div(rel, 2) - 2 * lax.div(rel, 3)

    slots = [slot_of(s) for s in range(4)]
    rest = [pred[slots[s]].reshape(128, 256) for s in range(4)]
    for s in range(3, -1, -1):
        w = jnp.dot(mref[slots[s]], rest[s], precision=HIGHEST)
        h, l = split(w)
        at = pl.ds(pl.multiple_of(slots[s] * 128, 128), 128)
        wh_ref[at] = h
        wl_ref[at] = l
        for r in range(s):
            rest[r] = rest[r] - jnp.dot(gf[slots[r], slots[s]], w, precision=HIGHEST)

    def sent(c, _):
        for way in range(2):
            z_own(way, c).wait_send()
        for slot in range(4):
            to_sib(slot, c).wait_send()
        for copy in store_out(c):
            copy.wait()
        return 0

    lax.fori_loop(0, CHUNKS, sent, 0)
    for j in range(CHUNKS // 2):
        z_pass(0, j).wait_send()
        z_pass(1, j).wait_send()
    for i in range(4):
        gx(i).wait_send()

    def sent_d(d):
        for kind in range(3):
            rs(kind, d).wait_send()
            ag_send(kind, d).wait_send()

    each(sent_d)


def update_kernel(x_ref, vh_ref, vl_ref, wh_ref, wl_ref, o_ref):
    o_ref[...] = x_ref[...] - dot3((vh_ref[0], vl_ref[0]), (wh_ref[...], wl_ref[...]))


def on_device(rows, eigenvectors, reflectors, triangles):
    height, width = eigenvectors.shape
    lanes = height // CHUNKS
    half = reflectors.shape[1]
    dma = pltpu.SemaphoreType.DMA
    anywhere = pl.BlockSpec(memory_space=pl.ANY)
    vmem = pl.BlockSpec(memory_space=pltpu.VMEM)
    wh, wl, vnh, vnl = pl.pallas_call(
        functools.partial(gather_kernel, rows),
        out_shape=[
            jax.ShapeDtypeStruct((512, width), BF16),
            jax.ShapeDtypeStruct((512, width), BF16),
            jax.ShapeDtypeStruct((CHUNKS, lanes, 512), BF16),
            jax.ShapeDtypeStruct((CHUNKS, lanes, 512), BF16),
        ],
        in_specs=[anywhere, anywhere, vmem],
        out_specs=[vmem, vmem, anywhere, anywhere],
        scratch_shapes=[
            pltpu.VMEM((4, CHUNKS, 2, half, lanes), F32),
            pltpu.VMEM((CHUNKS, lanes, width), F32),
            pltpu.VMEM((CHUNKS, lanes, width), BF16),
            pltpu.VMEM((CHUNKS, lanes, width), BF16),
            pltpu.VMEM((CHUNKS, lanes, 512), BF16),
            pltpu.VMEM((CHUNKS, lanes, 512), BF16),
            pltpu.VMEM((4, 16, 8, width), F32),
            pltpu.VMEM((4, 16, 8, width), F32),
            pltpu.VMEM((48, 8, 128), F32),
            pltpu.VMEM((2, 80, 8, 128), F32),
            pltpu.VMEM((4, 4, 128, 128), F32),
            pltpu.VMEM((4, 128, 128), F32),
            pltpu.VMEM((16, 3, 8, width), F32),
            pltpu.VMEM((16, 3, 8, 128), F32),
            pltpu.VMEM((16, 1, 8, width), F32),
            dma((CHUNKS,)), dma((CHUNKS,)),
            dma((4, CHUNKS)), dma((4, CHUNKS)),
            dma((2, CHUNKS + CHUNKS // 2)), dma((2, CHUNKS + CHUNKS // 2)),
            dma((3, 16)), dma((3, 16)), dma((3, 16)), dma((3, 16)),
            dma((4,)), dma((4,)), dma((2, CHUNKS)),
        ],
        compiler_params=pltpu.CompilerParams(
            collective_id=0, has_side_effects=True, vmem_limit_bytes=56 * 2**20),
    )(reflectors.T, eigenvectors, triangles)
    whole = pl.BlockSpec((512, width), lambda i: (0, 0))
    tall = pl.BlockSpec((1, lanes, 512), lambda i: (i, 0, 0))
    rowwise = pl.BlockSpec((lanes, width), lambda i: (i, 0))
    return pl.pallas_call(
        update_kernel,
        grid=(CHUNKS,),
        out_shape=jax.ShapeDtypeStruct((height, width), F32),
        in_specs=[rowwise, tall, tall, whole, whole],
        out_specs=rowwise,
        compiler_params=pltpu.CompilerParams(vmem_limit_bytes=32 * 2**20),
    )(eigenvectors, vnh, vnl, wh, wl)


def solution(mesh):
    return jax.shard_map(
        functools.partial(on_device, mesh.shape["row"]),
        mesh=mesh,
        in_specs=(P("row", "col"), P("row", "col"), P()),
        out_specs=P("row", "col"),
        check_vma=False,
    )
```

```python
import functools

import jax
import jax.numpy as jnp
from jax import lax
from jax.experimental import pallas as pl
from jax.experimental.pallas import tpu as pltpu
from jax.sharding import PartitionSpec as P

MESH = pl.DeviceIdType.MESH
HIGHEST = lax.Precision.HIGHEST
F32, BF16 = jnp.float32, jnp.bfloat16
CHUNKS = 8
OWN, UP, DOWN, FAR = range(4)
REL = (0, 1, 3, 2)
GRAM = ((OWN, UP), (UP, UP), (OWN, DOWN), (UP, DOWN), (OWN, OWN), (DOWN, DOWN),
        (UP, FAR), (FAR, FAR), (DOWN, FAR), (OWN, FAR))


def split(a):
    high = a.astype(BF16)
    return high, (a - high.astype(F32)).astype(BF16)


def dot3(a, b, dims=(((1,), (0,)), ((), ()))):
    d = functools.partial(lax.dot_general, dimension_numbers=dims, preferred_element_type=F32)
    return d(a[0], b[0]) + (d(a[0], b[1]) + d(a[1], b[0]))


NT = (((1,), (1,)), ((), ()))


def gather_kernel(rows, vt_in, x_in, t_ref, wh_ref, wl_ref, vnh, vnl, xb,
                  vt, xh, xl, pacc, pred, gacc, gh, gf, mref,
                  rs_e, rs_g, rs_l,
                  lsem, xsem, sbs, sbr, zs, zr, rss, rsr, ags, agr, gxs, gxr):
    me = lax.axis_index("row")
    col = lax.axis_index("col")
    z, k = lax.div(col, 2), lax.rem(col, 2)
    up = lax.rem(z + 1, 4) * 2 + k
    down = lax.rem(z + 3, 4) * 2 + k
    sib = z * 2 + 1 - k
    lanes = vt.shape[-1]

    barrier = pltpu.get_barrier_semaphore()
    for other in (up, down, sib):
        pl.semaphore_signal(barrier, inc=1, device_id=(me, other), device_id_type=MESH)
    for d in range(1, rows):
        pl.semaphore_signal(barrier, inc=1, device_id=(lax.rem(me + d, rows), col), device_id_type=MESH)

    def own(c):
        return vt_in.at[:, pl.ds(pl.multiple_of(c * lanes, lanes), lanes)]

    def local(c):
        return pltpu.make_async_copy(own(c), vt.at[OWN, c, k], lsem.at[c])

    def load_x(c):
        return pltpu.make_async_copy(x_in.at[pl.ds(pl.multiple_of(c * lanes, lanes), lanes)], xb.at[c], xsem.at[c])

    def remote(src, dst, ssem, rsem, target):
        return pltpu.make_async_remote_copy(src_ref=src, dst_ref=dst, send_sem=ssem, recv_sem=rsem,
                                            device_id=target, device_id_type=MESH)

    def z_own(way, c):
        return remote(own(c), vt.at[(UP, DOWN)[way], c, k], zs.at[way, c], zr.at[way, c], (me, (down, up)[way]))

    def z_pass(way, j):
        c = (j, CHUNKS // 2 + j)[way]
        return remote(vt.at[(UP, DOWN)[way], c, k], vt.at[FAR, c, k],
                      zs.at[way, CHUNKS + j], zr.at[way, CHUNKS + j], (me, (down, up)[way]))

    def to_sib(slot, c):
        src = own(c) if slot == OWN else vt.at[slot, c, k]
        return remote(src, vt.at[slot, c, k], sbs.at[slot, c], sbr.at[slot, c], (me, sib))

    def peer(d):
        return lax.rem(me + d, rows)

    def rs(kind, d):
        p = peer(d)
        src = (pacc.at[pl.ds(0, 3), p], gacc.at[pl.ds(3 * p, 3)], pacc.at[pl.ds(3, 1), p])[kind]
        dst = (rs_e, rs_g, rs_l)[kind].at[d]
        return remote(src, dst, rss.at[kind, d], rsr.at[kind, d], (p, col))

    def piece(kind, owner):
        return (pred.at[pl.ds(0, 3), owner], gh.at[k, pl.ds(3 * owner, 3)], pred.at[pl.ds(3, 1), owner])[kind]

    def ag_send(kind, d):
        return remote(piece(kind, me), piece(kind, me), ags.at[kind, d], agr.at[kind, d], (peer(d), col))

    def ag_recv(kind, d):
        source = lax.rem(me + rows - d, rows)
        return remote(piece(kind, source), piece(kind, source), ags.at[kind, d], agr.at[kind, d], (peer(d), col))

    def each(fn):
        lax.fori_loop(1, rows, lambda d, _: (fn(d), 0)[1], 0)

    def reduce_scatter(kind):
        each(lambda d: rs(kind, d).start())

    def sum_and_gather(kind):
        each(lambda d: rs(kind, d).wait_recv())
        buf = (rs_e, rs_g, rs_l)[kind]
        total = (pacc[0:3, me], gacc[pl.ds(3 * me, 3)], pacc[3:4, me])[kind]
        for d in range(1, rows):
            total = total + buf[d]
        if kind == 1:
            gh[k, pl.ds(3 * me, 3)] = total
        elif kind == 0:
            pred[0:3, me] = total
        else:
            pred[3:4, me] = total
        each(lambda d: ag_send(kind, d).start())

    def finish_gather(kind):
        each(lambda d: ag_recv(kind, d).wait_recv())

    def gx(i):
        half = pl.ds(0, 48)
        if i == 0:
            return remote(gh.at[k, pl.ds(0, 16)], gh.at[k, pl.ds(48, 16)], gxs.at[0], gxr.at[0], (me, down))
        if i == 1:
            return remote(gh.at[k, pl.ds(16, 16)], gh.at[k, pl.ds(64, 16)], gxs.at[1], gxr.at[1], (me, up))
        if i == 3:
            half = pl.ds(48, 32)
        return remote(gh.at[k, half], gh.at[k, half], gxs.at[i], gxr.at[i], (me, sib))

    def block(slot, c):
        return vt[slot, c].reshape(2 * vt.shape[3], lanes)

    def apply(slot, c, first):
        v = block(slot, c)
        p = dot3(split(v), (xh[c], xl[c])).reshape(16, 8, 256)
        th, tl = split(v.T)
        vnh[c, :, slot * 128:(slot + 1) * 128] = th
        vnl[c, :, slot * 128:(slot + 1) * 128] = tl
        pacc[slot] += p

    def gram(c):
        v = [split(block(s, c)) for s in (OWN, UP, DOWN)]
        a = [split(vt[s, c, k]) for s in (OWN, UP, DOWN)]
        for i, (r, s) in enumerate(GRAM[:6]):
            gacc[8 * i:8 * i + 8] += dot3(a[r], v[s], NT).reshape(8, 8, 128)

    for c in range(CHUNKS):
        local(c).start()
        load_x(c).start()
    pl.semaphore_wait(barrier, rows + 2)
    for c in range(2):
        for way in range(2):
            z_own(way, c).start()
    for c in range(CHUNKS):
        to_sib(OWN, c).start()
    pacc[...] = jnp.zeros_like(pacc)
    gacc[...] = jnp.zeros_like(gacc)

    def neighbours(c):
        to_sib(UP, c).wait_recv()
        to_sib(DOWN, c).wait_recv()
        apply(UP, c, False)
        apply(DOWN, c, False)
        gram(c)

    def step(c, _):
        load_x(c).wait()
        h, l = split(xb[c])
        xh[c] = h
        xl[c] = l
        local(c).wait()
        to_sib(OWN, c).wait_recv()
        apply(OWN, c, False)

        @pl.when(c > 0)
        def _():
            neighbours(c - 1)

        z_own(0, c).wait_recv()
        z_own(1, c).wait_recv()

        @pl.when(c < CHUNKS - 2)
        def _():
            z_own(0, c + 2).start()
            z_own(1, c + 2).start()

        @pl.when(c >= CHUNKS - 2)
        def _():
            for i in range(2):
                j = 2 * (c - (CHUNKS - 2)) + i
                z_pass(0, j).start()
                z_pass(1, j).start()

        to_sib(UP, c).start()
        to_sib(DOWN, c).start()
        return 0

    lax.fori_loop(0, CHUNKS, step, 0)

    def far(j):
        def one(i, _):
            c = j + i * (CHUNKS // 2)
            to_sib(FAR, c).wait_recv()
            apply(FAR, c, True)
            return 0
        lax.fori_loop(0, 2, one, 0)

    def arrived(j):
        z_pass(0, j).wait_recv()
        z_pass(1, j).wait_recv()
        to_sib(FAR, j).start()
        to_sib(FAR, CHUNKS // 2 + j).start()

    neighbours(CHUNKS - 1)
    reduce_scatter(1)
    reduce_scatter(0)
    arrived(0)
    sum_and_gather(1)
    far(0)
    arrived(1)
    sum_and_gather(0)
    finish_gather(1)
    for i in range(3):
        gx(i).start()
    far(1)
    arrived(2)
    gx(0).wait_recv()
    gx(1).wait_recv()
    gx(3).start()
    far(2)
    arrived(3)
    far(3)
    reduce_scatter(2)
    gx(2).wait_recv()
    gx(3).wait_recv()
    for i, (r, s) in enumerate(GRAM):
        full = gh[:, 8 * i:8 * i + 8].reshape(128, 128)
        gf[r, s] = full
        if r != s:
            gf[s, r] = full.T
    mref[...] = jnp.zeros_like(mref)
    at_row = lax.broadcasted_iota(jnp.int32, (32, 128), 0)
    at_col = lax.broadcasted_iota(jnp.int32, (32, 128), 1)
    for i in range(3, -1, -1):
        part = slice(32 * i, 32 * i + 32)
        unit = jnp.where(at_col == at_row + 32 * i, 1.0, 0.0).astype(F32)
        for slot in range(4):
            shard = lax.rem(z + REL[slot], 4)
            rest = unit - jnp.dot(gf[slot, slot, part, :], mref[slot], precision=HIGHEST)
            mref[slot, part, :] = jnp.dot(t_ref[4 * shard + i], rest, precision=HIGHEST)
    sum_and_gather(2)
    finish_gather(0)
    finish_gather(2)

    def slot_of(shard):
        rel = lax.rem(shard - z + 4, 4)
        return rel + lax.div(rel, 2) - 2 * lax.div(rel, 3)

    slots = [slot_of(s) for s in range(4)]
    rest = [pred[slots[s]].reshape(128, 256) for s in range(4)]
    for s in range(3, -1, -1):
        w = jnp.dot(mref[slots[s]], rest[s], precision=HIGHEST)
        h, l = split(w)
        at = pl.ds(pl.multiple_of(slots[s] * 128, 128), 128)
        wh_ref[at] = h
        wl_ref[at] = l
        for r in range(s):
            rest[r] = rest[r] - jnp.dot(gf[slots[r], slots[s]], w, precision=HIGHEST)

    def sent(c, _):
        for way in range(2):
            z_own(way, c).wait_send()
        for slot in range(4):
            to_sib(slot, c).wait_send()
        return 0

    lax.fori_loop(0, CHUNKS, sent, 0)
    for j in range(CHUNKS // 2):
        z_pass(0, j).wait_send()
        z_pass(1, j).wait_send()
    for i in range(4):
        gx(i).wait_send()

    def sent_d(d):
        for kind in range(3):
            rs(kind, d).wait_send()
            ag_send(kind, d).wait_send()

    each(sent_d)


def update_kernel(xb, vnh, vnl, wh_ref, wl_ref, out, buf, sem):
    lanes = buf.shape[1]
    w = wh_ref[...], wl_ref[...]

    def store(c):
        return pltpu.make_async_copy(buf.at[c], out.at[pl.ds(pl.multiple_of(c * lanes, lanes), lanes)], sem.at[c])

    def one(c, _):
        buf[c] = xb[c] - dot3((vnh[c], vnl[c]), w)
        store(c).start()
        return 0

    lax.fori_loop(0, CHUNKS, one, 0)
    lax.fori_loop(0, CHUNKS, lambda c, _: (store(c).wait(), 0)[1], 0)


def on_device(rows, eigenvectors, reflectors, triangles):
    height, width = eigenvectors.shape
    lanes = height // CHUNKS
    half = reflectors.shape[1]
    dma = pltpu.SemaphoreType.DMA
    anywhere = pl.BlockSpec(memory_space=pl.ANY)
    vmem = pl.BlockSpec(memory_space=pltpu.VMEM)
    wh, wl, vnh, vnl, xb = pl.pallas_call(
        functools.partial(gather_kernel, rows),
        out_shape=[
            pltpu.VMEM((512, width), BF16),
            pltpu.VMEM((512, width), BF16),
            pltpu.VMEM((CHUNKS, lanes, 512), BF16),
            pltpu.VMEM((CHUNKS, lanes, 512), BF16),
            pltpu.VMEM((CHUNKS, lanes, width), F32),
        ],
        in_specs=[anywhere, anywhere, vmem],
        out_specs=[vmem] * 5,
        scratch_shapes=[
            pltpu.VMEM((4, CHUNKS, 2, half, lanes), F32),
            pltpu.VMEM((CHUNKS, lanes, width), BF16),
            pltpu.VMEM((CHUNKS, lanes, width), BF16),
            pltpu.VMEM((4, 16, 8, width), F32),
            pltpu.VMEM((4, 16, 8, width), F32),
            pltpu.VMEM((48, 8, 128), F32),
            pltpu.VMEM((2, 80, 8, 128), F32),
            pltpu.VMEM((4, 4, 128, 128), F32),
            pltpu.VMEM((4, 128, 128), F32),
            pltpu.VMEM((16, 3, 8, width), F32),
            pltpu.VMEM((16, 3, 8, 128), F32),
            pltpu.VMEM((16, 1, 8, width), F32),
            dma((CHUNKS,)), dma((CHUNKS,)),
            dma((4, CHUNKS)), dma((4, CHUNKS)),
            dma((2, CHUNKS + CHUNKS // 2)), dma((2, CHUNKS + CHUNKS // 2)),
            dma((3, 16)), dma((3, 16)), dma((3, 16)), dma((3, 16)),
            dma((4,)), dma((4,)),
        ],
        compiler_params=pltpu.CompilerParams(
            collective_id=0, has_side_effects=True, vmem_limit_bytes=36 * 2**20),
    )(reflectors.T, eigenvectors, triangles)
    return pl.pallas_call(
        update_kernel,
        out_shape=jax.ShapeDtypeStruct((height, width), F32),
        in_specs=[vmem] * 5,
        out_specs=anywhere,
        scratch_shapes=[pltpu.VMEM((CHUNKS, lanes, width), F32), dma((CHUNKS,))],
        compiler_params=pltpu.CompilerParams(vmem_limit_bytes=16 * 2**20),
    )(xb, vnh, vnl, wh, wl)


def solution(mesh):
    return jax.shard_map(
        functools.partial(on_device, mesh.shape["row"]),
        mesh=mesh,
        in_specs=(P("row", "col"), P("row", "col"), P()),
        out_specs=P("row", "col"),
        check_vma=False,
    )
```

```python
import functools

import jax
import jax.numpy as jnp
from jax import lax
from jax.experimental import pallas as pl
from jax.experimental.pallas import tpu as pltpu
from jax.sharding import PartitionSpec as P

MESH = pl.DeviceIdType.MESH
F32, BF16 = jnp.float32, jnp.bfloat16
CHUNKS = 8
NEAR_SPLIT = 4
OWN, UP, DOWN, FAR = range(4)
REL = (0, 1, 3, 2)
GRAM = ((OWN, UP), (UP, UP), (OWN, DOWN), (UP, DOWN), (OWN, OWN), (DOWN, DOWN),
        (UP, FAR), (FAR, FAR), (DOWN, FAR), (OWN, FAR))


def split(a):
    high = a.astype(BF16)
    return high, (a - high.astype(F32)).astype(BF16)


def dot3(a, b, dims=(((1,), (0,)), ((), ()))):
    left = jnp.concatenate([a[0], a[0], a[1]], dims[0][0][0])
    right = jnp.concatenate([b[0], b[1], b[0]], dims[0][1][0])
    return lax.dot_general(left, right, dims, preferred_element_type=F32)


NT = (((1,), (1,)), ((), ()))


def dot(a, b):
    return dot3(split(a), split(b))


def gather_kernel(rows, vt_in, x_in, t_ref, rh_ref, rl_ref, vk, xb,
                  vt, xh, xl, vnh, vnl, wh, wl, wf, kh, kl, tb, pacc, pred, pred_l, gacc, gh, gf, mref,
                  rs_e, rs_g, rs_l,
                  xsem, own_in, near_in, far_in_sem, z_in, sib_out, z_out, rss, rsr, ags, agr, gxs, gxr, vks, vkr):
    me = lax.axis_index("row")
    col = lax.axis_index("col")
    z, k = lax.div(col, 2), lax.rem(col, 2)
    up = lax.rem(z + 1, 4) * 2 + k
    down = lax.rem(z + 3, 4) * 2 + k
    sib = z * 2 + 1 - k
    lanes = vt.shape[-1]

    barrier = pltpu.get_barrier_semaphore()
    for other in (up, down, sib):
        pl.semaphore_signal(barrier, inc=1, device_id=(me, other), device_id_type=MESH)
    for d in range(1, rows):
        pl.semaphore_signal(barrier, inc=1, device_id=(lax.rem(me + d, rows), col), device_id_type=MESH)

    def own(c):
        return vt_in.at[:, pl.ds(pl.multiple_of(c * lanes, lanes), lanes)]

    def local(c):
        return pltpu.make_async_copy(own(c), vt.at[OWN, c, k], own_in.at[c])

    def load_x(c):
        return pltpu.make_async_copy(x_in.at[pl.ds(pl.multiple_of(c * lanes, lanes), lanes)], xb.at[c], xsem.at[c])

    def remote(src, dst, ssem, rsem, target):
        return pltpu.make_async_remote_copy(src_ref=src, dst_ref=dst, send_sem=ssem, recv_sem=rsem,
                                            device_id=target, device_id_type=MESH)

    def z_own(way, c):
        return remote(own(c), vt.at[(UP, DOWN)[way], c, k], z_out, z_in.at[c], (me, (down, up)[way]))

    def z_pass(way, j):
        c = (j, CHUNKS // 2 + j)[way]
        return remote(vt.at[(UP, DOWN)[way], c, k], vt.at[FAR, c, k],
                      z_out, z_in.at[CHUNKS + j], (me, (down, up)[way]))

    def to_sib(slot, c):
        src = own(c) if slot == OWN else vt.at[slot, c, k]
        arrival = own_in.at[c] if slot == OWN else far_in_sem.at[lax.rem(c, CHUNKS // 2)] if slot == FAR else near_in.at[c]
        return remote(src, vt.at[slot, c, k], sib_out, arrival, (me, sib))

    def all_of(ref, sem):
        pltpu.make_async_copy(ref, ref, sem).wait()

    def peer(d):
        return lax.rem(me + d, rows)

    def rs(kind, d):
        p = peer(d)
        src = (pacc.at[pl.ds(0, 3), p], gacc.at[pl.ds(3 * p, 3)], pacc.at[pl.ds(3, 1), p])[kind]
        dst = (rs_e, rs_g, rs_l)[kind].at[d]
        return remote(src, dst, rss.at[kind], rsr.at[kind], (p, col))

    def piece(kind, owner):
        return (pred.at[pl.ds(0, 3), owner], gh.at[k, pl.ds(3 * owner, 3)], pred_l.at[pl.ds(0, 1), owner])[kind]

    def ag_send(kind, d):
        return remote(piece(kind, me), piece(kind, me), ags.at[kind], agr.at[kind], (peer(d), col))

    def others(kind):
        n = rows - 1
        return (rs_e.at[pl.ds(1, n)], rs_g.at[pl.ds(1, n)], rs_l.at[pl.ds(1, n)])[kind]

    def each(fn):
        lax.fori_loop(1, rows, lambda d, _: (fn(d), 0)[1], 0)

    def reduce_scatter(kind):
        each(lambda d: rs(kind, d).start())

    def sum_and_gather(kind):
        all_of(others(kind), rsr.at[kind])
        buf = (rs_e, rs_g, rs_l)[kind]
        total = (pacc[0:3, me], gacc[pl.ds(3 * me, 3)], pacc[3:4, me])[kind]
        for d in range(1, rows):
            total = total + buf[d]
        if kind == 1:
            gh[k, pl.ds(3 * me, 3)] = total
        elif kind == 0:
            pred[0:3, me] = total
        else:
            pred_l[0:1, me] = total
        each(lambda d: ag_send(kind, d).start())

    def finish_gather(kind):
        all_of(others(kind), agr.at[kind])

    def gx(i):
        half = pl.ds(0, 48)
        if i == 0:
            return remote(gh.at[k, pl.ds(0, 16)], gh.at[k, pl.ds(48, 16)], gxs.at[0], gxr.at[0], (me, down))
        if i == 1:
            return remote(gh.at[k, pl.ds(16, 16)], gh.at[k, pl.ds(64, 16)], gxs.at[1], gxr.at[1], (me, up))
        if i == 3:
            half = pl.ds(48, 32)
        return remote(gh.at[k, half], gh.at[k, half], gxs.at[i], gxr.at[i], (me, sib))

    def block(slot, c):
        return vt[slot, c].reshape(2 * vt.shape[3], lanes)

    def multiply(slot, c):
        pacc[slot] += dot3(split(block(slot, c)), (xh[c], xl[c])).reshape(16, 8, 256)

    def upright(slot, c):
        th, tl = split(block(slot, c).T)
        vnh[c, :, slot * 128:(slot + 1) * 128] = th
        vnl[c, :, slot * 128:(slot + 1) * 128] = tl

    def apply(slot, c):
        multiply(slot, c)
        upright(slot, c)

    def gram(c):
        v = [split(block(s, c)) for s in (OWN, UP, DOWN)]
        a = [split(vt[s, c, k]) for s in (OWN, UP, DOWN)]
        for i, (r, s) in enumerate(GRAM[:6]):
            gacc[8 * i:8 * i + 8] += dot3(a[r], v[s], NT).reshape(8, 8, 128)

    for c in range(CHUNKS):
        local(c).start()
        load_x(c).start()
    pl.semaphore_wait(barrier, rows + 2)
    for c in range(2):
        for way in range(2):
            z_own(way, c).start()
    for c in range(CHUNKS):
        to_sib(OWN, c).start()
    pacc[...] = jnp.zeros_like(pacc)
    gacc[...] = jnp.zeros_like(gacc)
    gf[...] = jnp.zeros_like(gf)
    mref[...] = jnp.zeros_like(mref)
    pred[3] = jnp.zeros_like(pred[3])
    tb[...] = jnp.zeros_like(tb)
    for slot in range(4):
        shard = lax.rem(z + REL[slot], 4)
        for i in range(4):
            tb[slot, 32 * i:32 * i + 32, 32 * i:32 * i + 32] = t_ref[4 * shard + i]

    def neighbours(c):
        all_of(vt.at[pl.ds(UP, 2), c, 1 - k], near_in.at[c])
        apply(UP, c)
        apply(DOWN, c)
        gram(c)

    def step(c, _):
        load_x(c).wait()
        h, l = split(xb[c])
        xh[c] = h
        xl[c] = l
        all_of(vt.at[OWN, c], own_in.at[c])
        apply(OWN, c)

        @pl.when(c > 0)
        def _():
            neighbours(c - 1)

        all_of(vt.at[pl.ds(UP, 2), c, k], z_in.at[c])

        @pl.when(c < CHUNKS - 2)
        def _():
            z_own(0, c + 2).start()
            z_own(1, c + 2).start()

        @pl.when(c >= CHUNKS - 2)
        def _():
            for i in range(2):
                j = 2 * (c - (CHUNKS - 2)) + i
                z_pass(0, j).start()
                z_pass(1, j).start()

        to_sib(UP, c).start()
        to_sib(DOWN, c).start()
        return 0

    lax.fori_loop(0, CHUNKS, step, 0)

    def far(j, *parts):
        def one(i, _):
            c = j + i * (CHUNKS // 2)
            for part in parts:
                part(c)
            return 0
        if far_in in parts:
            all_of(vt.at[FAR, pl.ds(0, 2), 1 - k], far_in_sem.at[j])
        lax.fori_loop(0, 2, one, 0)

    def far_in(c):
        multiply(FAR, c)

    def far_up(c):
        upright(FAR, c)

    def arrived(j):
        all_of(vt.at[FAR, pl.ds(0, 2), k], z_in.at[CHUNKS + j])
        to_sib(FAR, j).start()
        to_sib(FAR, CHUNKS // 2 + j).start()

    def slot_of(shard):
        rel = lax.rem(shard - z + 4, 4)
        return rel + lax.div(rel, 2) - 2 * lax.div(rel, 3)

    slots = [slot_of(s) for s in range(4)]

    def at_slot(s):
        return pl.ds(pl.multiple_of(slots[s] * 128, 128), 128)

    def assemble(first, last):
        for i in range(first, last):
            r, s = GRAM[i]
            full = gh[:, 8 * i:8 * i + 8].reshape(128, 128)
            gf[r, s] = full
            if r != s:
                gf[s, r] = full.T

    def invert(*which):
        row = lax.broadcasted_iota(jnp.int32, (128, 128), 0)
        lane = lax.broadcasted_iota(jnp.int32, (128, 128), 1)
        unit = jnp.where(lane == row, 1.0, 0.0).astype(F32)
        above = lane - lax.rem(lane, 32) > row
        n = [dot(tb[s], jnp.where(above, gf[s, s], 0.0)) for s in which]
        square = [dot(m, m) for m in n]
        both = [dot(unit - m, unit + q) for m, q in zip(n, square)]
        for s, m in zip(which, both):
            mref[s] = dot(m, tb[s])

    def substitute(rest, put):
        for s in range(3, -1, -1):
            w = dot(mref[slots[s]], rest[s])
            put(s, w)
            for r in range(s):
                rest[r] = rest[r] - dot(gf[slots[r], slots[s]], w)

    def near_w():
        def put(s, w):
            h, l = split(w)
            wh[at_slot(s)] = h
            wl[at_slot(s)] = l
            wf[slots[s]] = w
        substitute([pred[slots[s]].reshape(128, 256) for s in range(4)], put)

    def far_k():
        row = lax.broadcasted_iota(jnp.int32, (128, 128), 0)
        unit = jnp.where(lax.broadcasted_iota(jnp.int32, (128, 128), 1) == row, 1.0, 0.0).astype(F32)

        def put(s, w):
            h, l = split(w)
            kh[at_slot(s)] = h
            kl[at_slot(s)] = l
        substitute([jnp.where(slots[s] == FAR, unit, 0.0) for s in range(4)], put)

    def far_known():
        total = jnp.zeros((128, 256), F32)
        for slot in (OWN, UP, DOWN):
            after = lax.rem(z + REL[slot], 4) > lax.rem(z + 2, 4)
            total += jnp.where(after, dot(gf[FAR, slot], wf[slot]), 0.0)
        return total

    def near_update(first, last):
        def one(c, _):
            xb[c] -= dot3((vnh[c, :, :384], vnl[c, :, :384]), (wh[:384], wl[:384]))
            return 0
        lax.fori_loop(first, last, one, 0)

    def columns(c):
        return remote(vk.at[c], vk.at[c], vks, vkr, (me, sib))

    def far_columns():
        def one(i, _):
            c = k * (CHUNKS // 2) + i
            vk[c] = dot3((vnh[c], vnl[c]), (kh[...], kl[...]))
            columns(c).start()
            return 0
        lax.fori_loop(0, CHUNKS // 2, one, 0)

    neighbours(CHUNKS - 1)
    reduce_scatter(1)
    reduce_scatter(0)
    arrived(0)
    far(0, far_in, far_up)
    sum_and_gather(1)
    sum_and_gather(0)
    arrived(1)
    far(1, far_in, far_up)
    finish_gather(1)
    for i in range(3):
        gx(i).start()
    arrived(2)
    far(2, far_in, far_up)
    gx(2).wait_recv()
    assemble(0, 6)
    invert(OWN, UP, DOWN)
    finish_gather(0)
    arrived(3)
    near_w()
    far(3, far_in)
    reduce_scatter(2)
    gx(0).wait_recv()
    gx(1).wait_recv()
    gx(3).start()
    far(3, far_up)
    near_update(0, NEAR_SPLIT)
    gx(3).wait_recv()
    assemble(6, 10)
    invert(FAR)
    far_k()
    sum_and_gather(2)
    far_columns()
    known = far_known()
    near_update(NEAR_SPLIT, CHUNKS)
    finish_gather(2)
    h, l = split(pred_l[0].reshape(128, 256) - known)
    rh_ref[...] = h
    rl_ref[...] = l

    all_of(vk.at[pl.ds(0, CHUNKS // 2)], vkr)
    all_of(vk.at[pl.ds(0, CHUNKS // 2)], vks)
    all_of(vt.at[:, :, 0], sib_out)
    all_of(vt.at[pl.ds(0, 3), :, 0], z_out)
    for i in range(4):
        gx(i).wait_send()
    for kind in range(3):
        all_of(others(kind), rss.at[kind])
        all_of(others(kind), ags.at[kind])


def update_kernel(xb, vk, rh_ref, rl_ref, out, buf, sem):
    lanes = buf.shape[1]
    r = rh_ref[...], rl_ref[...]

    def store(c):
        return pltpu.make_async_copy(buf.at[c], out.at[pl.ds(pl.multiple_of(c * lanes, lanes), lanes)], sem.at[c])

    def one(c, _):
        change = dot3(split(vk[c]), r)
        buf[c] = xb[c] - jnp.where(change == change, change, 0.0)
        store(c).start()
        return 0

    lax.fori_loop(0, CHUNKS, one, 0)
    lax.fori_loop(0, CHUNKS, lambda c, _: (store(c).wait(), 0)[1], 0)


def on_device(rows, eigenvectors, reflectors, triangles):
    height, width = eigenvectors.shape
    lanes = height // CHUNKS
    half = reflectors.shape[1]
    dma = pltpu.SemaphoreType.DMA
    anywhere = pl.BlockSpec(memory_space=pl.ANY)
    vmem = pl.BlockSpec(memory_space=pltpu.VMEM)
    rh, rl, vk, xb = pl.pallas_call(
        functools.partial(gather_kernel, rows),
        out_shape=[
            pltpu.VMEM((128, width), BF16),
            pltpu.VMEM((128, width), BF16),
            pltpu.VMEM((CHUNKS, lanes, 128), F32),
            pltpu.VMEM((CHUNKS, lanes, width), F32),
        ],
        in_specs=[anywhere, anywhere, vmem],
        out_specs=[vmem] * 4,
        scratch_shapes=[
            pltpu.VMEM((4, CHUNKS, 2, half, lanes), F32),
            pltpu.VMEM((CHUNKS, lanes, width), BF16),
            pltpu.VMEM((CHUNKS, lanes, width), BF16),
            pltpu.VMEM((CHUNKS, lanes, 512), BF16),
            pltpu.VMEM((CHUNKS, lanes, 512), BF16),
            pltpu.VMEM((512, width), BF16),
            pltpu.VMEM((512, width), BF16),
            pltpu.VMEM((4, 128, width), F32),
            pltpu.VMEM((512, 128), BF16),
            pltpu.VMEM((512, 128), BF16),
            pltpu.VMEM((4, 128, 128), F32),
            pltpu.VMEM((4, 16, 8, width), F32),
            pltpu.VMEM((4, 16, 8, width), F32),
            pltpu.VMEM((1, 16, 8, width), F32),
            pltpu.VMEM((48, 8, 128), F32),
            pltpu.VMEM((2, 80, 8, 128), F32),
            pltpu.VMEM((4, 4, 128, 128), F32),
            pltpu.VMEM((4, 128, 128), F32),
            pltpu.VMEM((16, 3, 8, width), F32),
            pltpu.VMEM((16, 3, 8, 128), F32),
            pltpu.VMEM((16, 1, 8, width), F32),
            dma((CHUNKS,)), dma((CHUNKS,)), dma((CHUNKS,)), dma((CHUNKS // 2,)), dma((CHUNKS + CHUNKS // 2,)), dma, dma,
            dma((3,)), dma((3,)), dma((3,)), dma((3,)), dma((4,)), dma((4,)), dma, dma,
        ],
        compiler_params=pltpu.CompilerParams(
            collective_id=0, has_side_effects=True, vmem_limit_bytes=46 * 2**20),
    )(reflectors.T, eigenvectors, triangles)
    return pl.pallas_call(
        update_kernel,
        out_shape=jax.ShapeDtypeStruct((height, width), F32),
        in_specs=[vmem] * 4,
        out_specs=anywhere,
        scratch_shapes=[pltpu.VMEM((CHUNKS, lanes, width), F32), dma((CHUNKS,))],
        compiler_params=pltpu.CompilerParams(vmem_limit_bytes=16 * 2**20),
    )(xb, vk, rh, rl)


def solution(mesh):
    return jax.shard_map(
        functools.partial(on_device, mesh.shape["row"]),
        mesh=mesh,
        in_specs=(P("row", "col"), P("row", "col"), P()),
        out_specs=P("row", "col"),
        check_vma=False,
    )
```

```python
import functools

import jax
import jax.numpy as jnp
from jax import lax
from jax.experimental import pallas as pl
from jax.experimental.pallas import tpu as pltpu
from jax.sharding import PartitionSpec as P

MESH = pl.DeviceIdType.MESH
F32, BF16 = jnp.float32, jnp.bfloat16
CHUNKS = 8
SIDE = 4
OWN, UP, DOWN, FAR = range(4)
REL = (0, 1, 3, 2)
GRAM = ((OWN, UP), (UP, UP), (OWN, DOWN), (UP, DOWN), (OWN, OWN), (DOWN, DOWN),
        (UP, FAR), (FAR, FAR), (DOWN, FAR), (OWN, FAR))


def split(a):
    high = a.astype(BF16)
    return high, (a - high.astype(F32)).astype(BF16)


def dot3(a, b, dims=(((1,), (0,)), ((), ()))):
    left = jnp.concatenate([a[0], a[0], a[1]], dims[0][0][0])
    right = jnp.concatenate([b[0], b[1], b[0]], dims[0][1][0])
    return lax.dot_general(left, right, dims, preferred_element_type=F32)


NT = (((1,), (1,)), ((), ()))


def dot(a, b):
    return dot3(split(a), split(b))


def gather_kernel(rows, vt_in, x_in, t_ref, wh, wl, vnh, vnl, xb,
                  vt, xh, xl, wf, kh, kl, tb, pacc, pred, pred_l, gacc, gh, gf, mref,
                  rs_e, rs_g, rs_l, rs_o,
                  xsem, own_in, near_in, far_in_sem, z_in, sib_out, z_out, rss, rsr, ags, agr, gxs, gxr, line_in):
    me = lax.axis_index("row")
    col = lax.axis_index("col")
    z, k = lax.div(col, 2), lax.rem(col, 2)
    up = lax.rem(z + 1, 4) * 2 + k
    down = lax.rem(z + 3, 4) * 2 + k
    sib = z * 2 + 1 - k
    lanes = vt.shape[-1]

    barrier = pltpu.get_barrier_semaphore()
    for other in (up, down, sib):
        pl.semaphore_signal(barrier, inc=1, device_id=(me, other), device_id_type=MESH)
    across = [lax.rem(me + SIDE * d, rows) for d in range(1, SIDE)]
    along = [lax.div(me, SIDE) * SIDE + lax.rem(lax.rem(me, SIDE) + d, SIDE) for d in range(1, SIDE)]
    for other in across + along:
        pl.semaphore_signal(barrier, inc=1, device_id=(other, col), device_id_type=MESH)

    def own(c):
        return vt_in.at[:, pl.ds(pl.multiple_of(c * lanes, lanes), lanes)]

    def local(c):
        return pltpu.make_async_copy(own(c), vt.at[OWN, c, k], own_in.at[c])

    def load_x(c):
        return pltpu.make_async_copy(x_in.at[pl.ds(pl.multiple_of(c * lanes, lanes), lanes)], xb.at[c], xsem.at[c])

    def remote(src, dst, ssem, rsem, target):
        return pltpu.make_async_remote_copy(src_ref=src, dst_ref=dst, send_sem=ssem, recv_sem=rsem,
                                            device_id=target, device_id_type=MESH)

    def z_own(way, c):
        return remote(own(c), vt.at[(UP, DOWN)[way], c, k], z_out, z_in.at[c], (me, (down, up)[way]))

    def z_pass(way, j):
        c = (j, CHUNKS // 2 + j)[way]
        return remote(vt.at[(UP, DOWN)[way], c, k], vt.at[FAR, c, k],
                      z_out, z_in.at[CHUNKS + j], (me, (down, up)[way]))

    def to_sib(slot, c):
        src = own(c) if slot == OWN else vt.at[slot, c, k]
        arrival = own_in.at[c] if slot == OWN else far_in_sem.at[lax.rem(c, CHUNKS // 2)] if slot == FAR else near_in.at[c]
        return remote(src, vt.at[slot, c, k], sib_out, arrival, (me, sib))

    def all_of(ref, sem):
        pltpu.make_async_copy(ref, ref, sem).wait()

    def peer(d):
        return lax.rem(me + d, rows)

    def rs(kind, d):
        p = peer(d)
        src = (pacc.at[pl.ds(UP, 2), p], gacc.at[pl.ds(3 * p, 3)], pacc.at[pl.ds(FAR, 1), p], pacc.at[pl.ds(OWN, 1), p])[kind]
        dst = (rs_e, rs_g, rs_l, rs_o)[kind].at[d]
        return remote(src, dst, rss.at[kind], rsr.at[kind], (p, col))

    def piece(kind, owner):
        return (pred.at[pl.ds(UP, 2), owner], gh.at[k, pl.ds(3 * owner, 3)], pred_l.at[pl.ds(0, 1), owner],
                pred.at[pl.ds(OWN, 1), owner])[kind]

    def ag_send(kind, d):
        return remote(piece(kind, me), piece(kind, me), ags.at[kind], agr.at[kind], (peer(d), col))

    def others(kind):
        n = rows - 1
        return (rs_e, rs_g, rs_l, rs_o)[kind].at[pl.ds(1, n)]

    def each(fn):
        lax.fori_loop(1, rows, lambda d, _: (fn(d), 0)[1], 0)

    def reduce_scatter(kind):
        each(lambda d: rs(kind, d).start())

    def sum_and_gather(kind):
        all_of(others(kind), rsr.at[kind])
        buf = (rs_e, rs_g, rs_l, rs_o)[kind]
        total = (pacc[UP:UP + 2, me], gacc[pl.ds(3 * me, 3)], pacc[FAR:FAR + 1, me], pacc[OWN:OWN + 1, me])[kind]
        for d in range(1, rows):
            total = total + buf[d]
        if kind == 1:
            gh[k, pl.ds(3 * me, 3)] = total
        elif kind == 0:
            pred[UP:UP + 2, me] = total
        elif kind == 2:
            pred_l[0:1, me] = total
        else:
            pred[OWN:OWN + 1, me] = total
        each(lambda d: ag_send(kind, d).start())

    def finish_gather(kind):
        all_of(others(kind), agr.at[kind])

    def gx(i):
        half = pl.ds(0, 48)
        if i == 0:
            return remote(gh.at[k, pl.ds(0, 16)], gh.at[k, pl.ds(48, 16)], gxs.at[0], gxr.at[0], (me, down))
        if i == 1:
            return remote(gh.at[k, pl.ds(16, 16)], gh.at[k, pl.ds(64, 16)], gxs.at[1], gxr.at[1], (me, up))
        if i == 3:
            half = pl.ds(48, 32)
        return remote(gh.at[k, half], gh.at[k, half], gxs.at[i], gxr.at[i], (me, sib))

    def block(slot, c):
        return vt[slot, c].reshape(2 * vt.shape[3], lanes)

    def multiply(slot, c):
        pacc[slot] += dot3(split(block(slot, c)), (xh[c], xl[c])).reshape(16, 8, 256)

    def upright(slot, c):
        th, tl = split(block(slot, c).T)
        vnh[c, :, slot * 128:(slot + 1) * 128] = th
        vnl[c, :, slot * 128:(slot + 1) * 128] = tl

    def apply(slot, c):
        multiply(slot, c)
        upright(slot, c)

    def gram(c):
        v = [split(block(s, c)) for s in (OWN, UP, DOWN)]
        a = [split(vt[s, c, k]) for s in (OWN, UP, DOWN)]
        for i, (r, s) in enumerate(GRAM[:6]):
            gacc[8 * i:8 * i + 8] += dot3(a[r], v[s], NT).reshape(8, 8, 128)

    for c in range(CHUNKS):
        local(c).start()
        load_x(c).start()
    pl.semaphore_wait(barrier, 2 * SIDE + 1)
    for c in range(2):
        for way in range(2):
            z_own(way, c).start()
    for c in range(CHUNKS):
        to_sib(OWN, c).start()
    for other in across:
        pl.semaphore_signal(line_in, inc=1, device_id=(other, col), device_id_type=MESH)
    pacc[...] = jnp.zeros_like(pacc)
    gacc[...] = jnp.zeros_like(gacc)
    gf[...] = jnp.zeros_like(gf)
    mref[...] = jnp.zeros_like(mref)
    pred[3] = jnp.zeros_like(pred[3])
    tb[...] = jnp.zeros_like(tb)
    for slot in range(4):
        shard = lax.rem(z + REL[slot], 4)
        for i in range(4):
            tb[slot, 32 * i:32 * i + 32, 32 * i:32 * i + 32] = t_ref[4 * shard + i]

    def neighbours(c):
        all_of(vt.at[pl.ds(UP, 2), c, 1 - k], near_in.at[c])
        apply(UP, c)
        apply(DOWN, c)
        gram(c)

    def mine(c, _):
        load_x(c).wait()
        h, l = split(xb[c])
        xh[c] = h
        xl[c] = l
        all_of(vt.at[OWN, c], own_in.at[c])
        apply(OWN, c)
        return 0

    def step(c, _):
        @pl.when(c < CHUNKS // 2)
        def _():
            lax.fori_loop(2 * c, 2 * c + 2, mine, 0)

        @pl.when(c == CHUNKS // 2)
        def _():
            pl.semaphore_wait(line_in, SIDE - 1)
            reduce_scatter(3)

        @pl.when(c == CHUNKS - 2)
        def _():
            sum_and_gather(3)

        @pl.when(c > 0)
        def _():
            neighbours(c - 1)

        all_of(vt.at[pl.ds(UP, 2), c, k], z_in.at[c])

        @pl.when(c < CHUNKS - 2)
        def _():
            z_own(0, c + 2).start()
            z_own(1, c + 2).start()

        @pl.when(c >= CHUNKS - 2)
        def _():
            for i in range(2):
                j = 2 * (c - (CHUNKS - 2)) + i
                z_pass(0, j).start()
                z_pass(1, j).start()

        to_sib(UP, c).start()
        to_sib(DOWN, c).start()
        return 0

    lax.fori_loop(0, CHUNKS, step, 0)

    def far(j, *parts):
        def one(i, _):
            c = j + i * (CHUNKS // 2)
            for part in parts:
                part(c)
            return 0
        if far_in in parts:
            all_of(vt.at[FAR, pl.ds(0, 2), 1 - k], far_in_sem.at[j])
        lax.fori_loop(0, 2, one, 0)

    def far_in(c):
        multiply(FAR, c)

    def far_up(c):
        upright(FAR, c)

    def arrived(j):
        all_of(vt.at[FAR, pl.ds(0, 2), k], z_in.at[CHUNKS + j])
        to_sib(FAR, j).start()
        to_sib(FAR, CHUNKS // 2 + j).start()

    def slot_of(shard):
        rel = lax.rem(shard - z + 4, 4)
        return rel + lax.div(rel, 2) - 2 * lax.div(rel, 3)

    slots = [slot_of(s) for s in range(4)]

    def at_slot(s):
        return pl.ds(pl.multiple_of(slots[s] * 128, 128), 128)

    def assemble(first, last):
        for i in range(first, last):
            r, s = GRAM[i]
            full = gh[:, 8 * i:8 * i + 8].reshape(128, 128)
            gf[r, s] = full
            if r != s:
                gf[s, r] = full.T

    def invert(*which):
        row = lax.broadcasted_iota(jnp.int32, (128, 128), 0)
        lane = lax.broadcasted_iota(jnp.int32, (128, 128), 1)
        unit = jnp.where(lane == row, 1.0, 0.0).astype(F32)
        above = lane - lax.rem(lane, 32) > row
        n = [dot(tb[s], jnp.where(above, gf[s, s], 0.0)) for s in which]
        square = [dot(m, m) for m in n]
        both = [dot(unit - m, unit + q) for m, q in zip(n, square)]
        for s, m in zip(which, both):
            mref[s] = dot(m, tb[s])

    def substitute(rest, put):
        for s in range(3, -1, -1):
            w = dot(mref[slots[s]], rest[s])
            put(s, w)
            for r in range(s):
                rest[r] = rest[r] - dot(gf[slots[r], slots[s]], w)

    def near_w():
        def put(s, w):
            wf[slots[s]] = w
        substitute([pred[slots[s]].reshape(128, 256) for s in range(4)], put)

    def far_k():
        row = lax.broadcasted_iota(jnp.int32, (128, 128), 0)
        unit = jnp.where(lax.broadcasted_iota(jnp.int32, (128, 128), 1) == row, 1.0, 0.0).astype(F32)

        def put(s, w):
            h, l = split(w)
            kh[at_slot(s)] = h
            kl[at_slot(s)] = l
        substitute([jnp.where(slots[s] == FAR, unit, 0.0) for s in range(4)], put)

    def far_known():
        total = jnp.zeros((128, 256), F32)
        for slot in (OWN, UP, DOWN):
            after = lax.rem(z + REL[slot], 4) > lax.rem(z + 2, 4)
            total += jnp.where(after, dot(gf[FAR, slot], wf[slot]), 0.0)
        return total

    neighbours(CHUNKS - 1)
    reduce_scatter(1)
    reduce_scatter(0)
    arrived(0)
    far(0, far_in, far_up)
    sum_and_gather(1)
    arrived(1)
    far(1, far_in, far_up)
    sum_and_gather(0)
    arrived(2)
    far(2, far_in, far_up)
    finish_gather(1)
    for i in range(3):
        gx(i).start()
    arrived(3)
    far(3, far_in)
    reduce_scatter(2)
    far(3, far_up)
    gx(2).wait_recv()
    assemble(0, 6)
    invert(OWN, UP, DOWN)
    gx(0).wait_recv()
    gx(1).wait_recv()
    gx(3).start()
    sum_and_gather(2)
    finish_gather(3)
    finish_gather(0)
    near_w()
    gx(3).wait_recv()
    assemble(6, 10)
    invert(FAR)
    far_k()
    known = far_known()
    finish_gather(2)
    change = dot3((kh[...], kl[...]), split(pred_l[0].reshape(128, 256) - known))
    h, l = split(wf[...].reshape(512, 256) + jnp.where(change == change, change, 0.0))
    wh[...] = h
    wl[...] = l

    all_of(vt.at[:, :, 0], sib_out)
    all_of(vt.at[pl.ds(0, 3), :, 0], z_out)
    for i in range(4):
        gx(i).wait_send()
    for kind in range(4):
        all_of(others(kind), rss.at[kind])
        all_of(others(kind), ags.at[kind])


def update_kernel(xb, vnh, vnl, wh, wl, out, buf, sem):
    lanes = buf.shape[1]

    def store(c):
        return pltpu.make_async_copy(buf.at[c], out.at[pl.ds(pl.multiple_of(c * lanes, lanes), lanes)], sem.at[c])

    def one(c, _):
        buf[c] = xb[c] - dot3((vnh[c], vnl[c]), (wh[...], wl[...]))
        store(c).start()
        return 0

    lax.fori_loop(0, CHUNKS, one, 0, unroll=2)
    lax.fori_loop(0, CHUNKS, lambda c, _: (store(c).wait(), 0)[1], 0)


def on_device(rows, eigenvectors, reflectors, triangles):
    height, width = eigenvectors.shape
    lanes = height // CHUNKS
    half = reflectors.shape[1]
    dma = pltpu.SemaphoreType.DMA
    anywhere = pl.BlockSpec(memory_space=pl.ANY)
    vmem = pl.BlockSpec(memory_space=pltpu.VMEM)
    wh, wl, vnh, vnl, xb = pl.pallas_call(
        functools.partial(gather_kernel, rows),
        out_shape=[
            pltpu.VMEM((512, width), BF16),
            pltpu.VMEM((512, width), BF16),
            pltpu.VMEM((CHUNKS, lanes, 512), BF16),
            pltpu.VMEM((CHUNKS, lanes, 512), BF16),
            pltpu.VMEM((CHUNKS, lanes, width), F32),
        ],
        in_specs=[anywhere, anywhere, vmem],
        out_specs=[vmem] * 5,
        scratch_shapes=[
            pltpu.VMEM((4, CHUNKS, 2, half, lanes), F32),
            pltpu.VMEM((CHUNKS, lanes, width), BF16),
            pltpu.VMEM((CHUNKS, lanes, width), BF16),
            pltpu.VMEM((4, 128, width), F32),
            pltpu.VMEM((512, 128), BF16),
            pltpu.VMEM((512, 128), BF16),
            pltpu.VMEM((4, 128, 128), F32),
            pltpu.VMEM((4, 16, 8, width), F32),
            pltpu.VMEM((4, 16, 8, width), F32),
            pltpu.VMEM((1, 16, 8, width), F32),
            pltpu.VMEM((48, 8, 128), F32),
            pltpu.VMEM((2, 80, 8, 128), F32),
            pltpu.VMEM((4, 4, 128, 128), F32),
            pltpu.VMEM((4, 128, 128), F32),
            pltpu.VMEM((16, 2, 8, width), F32),
            pltpu.VMEM((16, 3, 8, 128), F32),
            pltpu.VMEM((16, 1, 8, width), F32),
            pltpu.VMEM((16, 1, 8, width), F32),
            dma((CHUNKS,)), dma((CHUNKS,)), dma((CHUNKS,)), dma((CHUNKS // 2,)), dma((CHUNKS + CHUNKS // 2,)), dma, dma,
            dma((4,)), dma((4,)), dma((4,)), dma((4,)), dma((4,)), dma((4,)), pltpu.SemaphoreType.REGULAR,
        ],
        compiler_params=pltpu.CompilerParams(
            collective_id=0, has_side_effects=True, vmem_limit_bytes=36 * 2**20),
    )(reflectors.T, eigenvectors, triangles)
    return pl.pallas_call(
        update_kernel,
        out_shape=jax.ShapeDtypeStruct((height, width), F32),
        in_specs=[vmem] * 5,
        out_specs=anywhere,
        scratch_shapes=[pltpu.VMEM((CHUNKS, lanes, width), F32), dma((CHUNKS,))],
        compiler_params=pltpu.CompilerParams(vmem_limit_bytes=16 * 2**20),
    )(xb, vnh, vnl, wh, wl)


def solution(mesh):
    return jax.shard_map(
        functools.partial(on_device, mesh.shape["row"]),
        mesh=mesh,
        in_specs=(P("row", "col"), P("row", "col"), P()),
        out_specs=P("row", "col"),
        check_vma=False,
    )
```

```python
import functools

import jax
import jax.numpy as jnp
from jax import lax
from jax.experimental import pallas as pl
from jax.experimental.pallas import tpu as pltpu
from jax.sharding import PartitionSpec as P

MESH = pl.DeviceIdType.MESH
F32, BF16 = jnp.float32, jnp.bfloat16
CHUNKS = 8
SIDE = 4
OWN, UP, DOWN, FAR = range(4)
REL = (0, 1, 3, 2)
GRAM = ((OWN, UP), (UP, UP), (OWN, DOWN), (UP, DOWN), (OWN, OWN), (DOWN, DOWN),
        (UP, FAR), (FAR, FAR), (DOWN, FAR), (OWN, FAR))


def split(a):
    high = a.astype(BF16)
    return high, (a - high.astype(F32)).astype(BF16)


def dot3(a, b, dims=(((1,), (0,)), ((), ()))):
    left = jnp.concatenate([a[0], a[0], a[1]], dims[0][0][0])
    right = jnp.concatenate([b[0], b[1], b[0]], dims[0][1][0])
    return lax.dot_general(left, right, dims, preferred_element_type=F32)


NT = (((1,), (1,)), ((), ()))


def dot(a, b):
    return dot3(split(a), split(b))


def gather_kernel(rows, vt_in, x_in, t_ref, wh, wl, vnh, vnl, xb,
                  vt, xh, xl, wf, kh, kl, tb, pacc, pred, pred_l, gacc, gh, gf, mref,
                  rs_e, rs_g, rs_l, rs_o,
                  xsem, own_in, near_in, far_in_sem, z_in, sib_out, z_out, rss, rsr, ags, agr, gxs, gxr, line_in):
    me = lax.axis_index("row")
    col = lax.axis_index("col")
    z, k = lax.div(col, 2), lax.rem(col, 2)
    up = lax.rem(z + 1, 4) * 2 + k
    down = lax.rem(z + 3, 4) * 2 + k
    sib = z * 2 + 1 - k
    lanes = vt.shape[-1]

    barrier = pltpu.get_barrier_semaphore()
    for other in (up, down, sib):
        pl.semaphore_signal(barrier, inc=1, device_id=(me, other), device_id_type=MESH)
    across = [lax.rem(me + SIDE * d, rows) for d in range(1, SIDE)]
    along = [lax.div(me, SIDE) * SIDE + lax.rem(lax.rem(me, SIDE) + d, SIDE) for d in range(1, SIDE)]
    for other in across + along:
        pl.semaphore_signal(barrier, inc=1, device_id=(other, col), device_id_type=MESH)

    def own(c):
        return vt_in.at[:, pl.ds(pl.multiple_of(c * lanes, lanes), lanes)]

    def local(c):
        return pltpu.make_async_copy(own(c), vt.at[OWN, c, k], own_in.at[c])

    def load_x(c):
        return pltpu.make_async_copy(x_in.at[pl.ds(pl.multiple_of(c * lanes, lanes), lanes)], xb.at[c], xsem.at[c])

    def remote(src, dst, ssem, rsem, target):
        return pltpu.make_async_remote_copy(src_ref=src, dst_ref=dst, send_sem=ssem, recv_sem=rsem,
                                            device_id=target, device_id_type=MESH)

    def z_own(way, c):
        return remote(own(c), vt.at[(UP, DOWN)[way], c, k], z_out, z_in.at[c], (me, (down, up)[way]))

    def z_pass(way, j):
        c = (j, CHUNKS // 2 + j)[way]
        return remote(vt.at[(UP, DOWN)[way], c, k], vt.at[FAR, c, k],
                      z_out, z_in.at[CHUNKS + j], (me, (down, up)[way]))

    def to_sib(slot, c):
        src = own(c) if slot == OWN else vt.at[slot, c, k]
        arrival = own_in.at[c] if slot == OWN else far_in_sem.at[lax.rem(c, CHUNKS // 2)] if slot == FAR else near_in.at[c]
        return remote(src, vt.at[slot, c, k], sib_out, arrival, (me, sib))

    def all_of(ref, sem):
        pltpu.make_async_copy(ref, ref, sem).wait()

    def peer(d):
        return lax.rem(me + d, rows)

    def rs(kind, d):
        p = peer(d)
        src = (pacc.at[pl.ds(UP, 2), p], gacc.at[pl.ds(3 * p, 3)], pacc.at[pl.ds(FAR, 1), p], pacc.at[pl.ds(OWN, 1), p])[kind]
        dst = (rs_e, rs_g, rs_l, rs_o)[kind].at[d]
        return remote(src, dst, rss.at[kind], rsr.at[kind], (p, col))

    def piece(kind, owner):
        return (pred.at[pl.ds(UP, 2), owner], gh.at[k, pl.ds(3 * owner, 3)], pred_l.at[pl.ds(0, 1), owner],
                pred.at[pl.ds(OWN, 1), owner])[kind]

    def ag_send(kind, d):
        return remote(piece(kind, me), piece(kind, me), ags.at[kind], agr.at[kind], (peer(d), col))

    def others(kind):
        n = rows - 1
        return (rs_e, rs_g, rs_l, rs_o)[kind].at[pl.ds(1, n)]

    def each(fn):
        lax.fori_loop(1, rows, lambda d, _: (fn(d), 0)[1], 0)

    def reduce_scatter(kind):
        each(lambda d: rs(kind, d).start())

    def sum_and_gather(kind):
        all_of(others(kind), rsr.at[kind])
        buf = (rs_e, rs_g, rs_l, rs_o)[kind]
        total = (pacc[UP:UP + 2, me], gacc[pl.ds(3 * me, 3)], pacc[FAR:FAR + 1, me], pacc[OWN:OWN + 1, me])[kind]
        for d in range(1, rows):
            total = total + buf[d]
        if kind == 1:
            gh[k, pl.ds(3 * me, 3)] = total
        elif kind == 0:
            pred[UP:UP + 2, me] = total
        elif kind == 2:
            pred_l[0:1, me] = total
        else:
            pred[OWN:OWN + 1, me] = total
        each(lambda d: ag_send(kind, d).start())

    def finish_gather(kind):
        all_of(others(kind), agr.at[kind])

    def gx(i):
        half = pl.ds(0, 48)
        if i == 0:
            return remote(gh.at[k, pl.ds(0, 16)], gh.at[k, pl.ds(48, 16)], gxs.at[0], gxr.at[0], (me, down))
        if i == 1:
            return remote(gh.at[k, pl.ds(16, 16)], gh.at[k, pl.ds(64, 16)], gxs.at[1], gxr.at[1], (me, up))
        if i == 3:
            half = pl.ds(48, 32)
        return remote(gh.at[k, half], gh.at[k, half], gxs.at[i], gxr.at[i], (me, sib))

    def block(slot, c):
        return vt[slot, c].reshape(2 * vt.shape[3], lanes)

    def multiply(slot, c):
        pacc[slot] += dot3(split(block(slot, c)), (xh[c], xl[c])).reshape(16, 8, 256)

    def upright(slot, c):
        th, tl = split(block(slot, c).T)
        vnh[c, :, slot * 128:(slot + 1) * 128] = th
        vnl[c, :, slot * 128:(slot + 1) * 128] = tl

    def apply(slot, c):
        multiply(slot, c)
        upright(slot, c)

    def gram(c):
        v = [split(block(s, c)) for s in (OWN, UP, DOWN)]
        a = [split(vt[s, c, k]) for s in (OWN, UP, DOWN)]
        for i, (r, s) in enumerate(GRAM[:6]):
            gacc[8 * i:8 * i + 8] += dot3(a[r], v[s], NT).reshape(8, 8, 128)

    for c in range(CHUNKS):
        local(c).start()
        load_x(c).start()
    pl.semaphore_wait(barrier, 2 * SIDE + 1)
    for c in range(2):
        for way in range(2):
            z_own(way, c).start()
    for c in range(CHUNKS):
        to_sib(OWN, c).start()
    for other in across:
        pl.semaphore_signal(line_in, inc=1, device_id=(other, col), device_id_type=MESH)
    pacc[...] = jnp.zeros_like(pacc)
    gacc[...] = jnp.zeros_like(gacc)
    gf[...] = jnp.zeros_like(gf)
    mref[...] = jnp.zeros_like(mref)
    pred[3] = jnp.zeros_like(pred[3])
    tb[...] = jnp.zeros_like(tb)
    for slot in range(4):
        shard = lax.rem(z + REL[slot], 4)
        for i in range(4):
            tb[slot, 32 * i:32 * i + 32, 32 * i:32 * i + 32] = t_ref[4 * shard + i]

    def neighbours(c):
        all_of(vt.at[pl.ds(UP, 2), c, 1 - k], near_in.at[c])
        apply(UP, c)
        apply(DOWN, c)
        gram(c)

    def mine(c, _):
        load_x(c).wait()
        h, l = split(xb[c])
        xh[c] = h
        xl[c] = l
        all_of(vt.at[OWN, c], own_in.at[c])
        apply(OWN, c)
        return 0

    def step(c, _):
        @pl.when(c < CHUNKS // 2)
        def _():
            lax.fori_loop(2 * c, 2 * c + 2, mine, 0)

        @pl.when(c == CHUNKS // 2)
        def _():
            pl.semaphore_wait(line_in, SIDE - 1)
            reduce_scatter(3)

        @pl.when(c == CHUNKS - 2)
        def _():
            sum_and_gather(3)

        @pl.when(c > 0)
        def _():
            neighbours(c - 1)

        all_of(vt.at[pl.ds(UP, 2), c, k], z_in.at[c])

        @pl.when(c < CHUNKS - 2)
        def _():
            z_own(0, c + 2).start()
            z_own(1, c + 2).start()

        @pl.when(c >= CHUNKS - 2)
        def _():
            for i in range(2):
                j = 2 * (c - (CHUNKS - 2)) + i
                z_pass(0, j).start()
                z_pass(1, j).start()

        to_sib(UP, c).start()
        to_sib(DOWN, c).start()
        return 0

    lax.fori_loop(0, CHUNKS, step, 0)

    def far(j, *parts):
        def one(i, _):
            c = j + i * (CHUNKS // 2)
            for part in parts:
                part(c)
            return 0
        if far_in in parts:
            all_of(vt.at[FAR, pl.ds(0, 2), 1 - k], far_in_sem.at[j])
        lax.fori_loop(0, 2, one, 0)

    def far_in(c):
        multiply(FAR, c)

    def far_up(c):
        upright(FAR, c)

    def arrived(j):
        all_of(vt.at[FAR, pl.ds(0, 2), k], z_in.at[CHUNKS + j])
        to_sib(FAR, j).start()
        to_sib(FAR, CHUNKS // 2 + j).start()

    def slot_of(shard):
        rel = lax.rem(shard - z + 4, 4)
        return rel + lax.div(rel, 2) - 2 * lax.div(rel, 3)

    slots = [slot_of(s) for s in range(4)]

    def at_slot(s):
        return pl.ds(pl.multiple_of(slots[s] * 128, 128), 128)

    def assemble(first, last):
        for i in range(first, last):
            r, s = GRAM[i]
            full = gh[:, 8 * i:8 * i + 8].reshape(128, 128)
            gf[r, s] = full
            if r != s:
                gf[s, r] = full.T

    def invert(*which):
        row = lax.broadcasted_iota(jnp.int32, (128, 128), 0)
        lane = lax.broadcasted_iota(jnp.int32, (128, 128), 1)
        unit = jnp.where(lane == row, 1.0, 0.0).astype(F32)
        above = lane - lax.rem(lane, 32) > row
        n = [dot(tb[s], jnp.where(above, gf[s, s], 0.0)) for s in which]
        square = [dot(m, m) for m in n]
        both = [dot(unit - m, unit + q) for m, q in zip(n, square)]
        for s, m in zip(which, both):
            mref[s] = dot(m, tb[s])

    def substitute(rest, put):
        for s in range(3, -1, -1):
            w = dot(mref[slots[s]], rest[s])
            put(s, w)
            for r in range(s):
                rest[r] = rest[r] - dot(gf[slots[r], slots[s]], w)

    def near_w():
        def put(s, w):
            wf[slots[s]] = w
        substitute([pred[slots[s]].reshape(128, 256) for s in range(4)], put)

    def far_k():
        row = lax.broadcasted_iota(jnp.int32, (128, 128), 0)
        unit = jnp.where(lax.broadcasted_iota(jnp.int32, (128, 128), 1) == row, 1.0, 0.0).astype(F32)

        def put(s, w):
            h, l = split(w)
            kh[at_slot(s)] = h
            kl[at_slot(s)] = l
        substitute([jnp.where(slots[s] == FAR, unit, 0.0) for s in range(4)], put)

    def far_known():
        total = jnp.zeros((128, 256), F32)
        for slot in (OWN, UP, DOWN):
            after = lax.rem(z + REL[slot], 4) > lax.rem(z + 2, 4)
            total += jnp.where(after, dot(gf[FAR, slot], wf[slot]), 0.0)
        return total

    neighbours(CHUNKS - 1)
    reduce_scatter(1)
    reduce_scatter(0)
    arrived(0)
    far(0, far_in, far_up)
    sum_and_gather(1)
    arrived(1)
    far(1, far_in, far_up)
    sum_and_gather(0)
    arrived(2)
    far(2, far_in, far_up)
    arrived(3)
    far(3, far_in)
    reduce_scatter(2)
    finish_gather(1)
    for i in range(3):
        gx(i).start()
    far(3, far_up)
    gx(2).wait_recv()
    assemble(0, 6)
    invert(OWN, UP, DOWN)
    gx(0).wait_recv()
    gx(1).wait_recv()
    gx(3).start()
    sum_and_gather(2)
    finish_gather(3)
    finish_gather(0)
    near_w()
    gx(3).wait_recv()
    assemble(6, 10)
    invert(FAR)
    far_k()
    known = far_known()
    finish_gather(2)
    change = dot3((kh[...], kl[...]), split(pred_l[0].reshape(128, 256) - known))
    h, l = split(wf[...].reshape(512, 256) + jnp.where(change == change, change, 0.0))
    wh[...] = h
    wl[...] = l

    all_of(vt.at[:, :, 0], sib_out)
    all_of(vt.at[pl.ds(0, 3), :, 0], z_out)
    for i in range(4):
        gx(i).wait_send()
    for kind in range(4):
        all_of(others(kind), rss.at[kind])
        all_of(others(kind), ags.at[kind])


def update_kernel(xb, vnh, vnl, wh, wl, out, buf, sem):
    lanes = buf.shape[1]

    def store(c):
        return pltpu.make_async_copy(buf.at[c], out.at[pl.ds(pl.multiple_of(c * lanes, lanes), lanes)], sem.at[c])

    def one(c, _):
        two = pl.ds(2 * c, 2)
        left = vnh[two].reshape(2 * lanes, 512), vnl[two].reshape(2 * lanes, 512)
        buf[two] = xb[two] - dot3(left, (wh[...], wl[...])).reshape(2, lanes, 256)
        store(2 * c).start()
        store(2 * c + 1).start()
        return 0

    lax.fori_loop(0, CHUNKS // 2, one, 0)
    lax.fori_loop(0, CHUNKS, lambda c, _: (store(c).wait(), 0)[1], 0)


def on_device(rows, eigenvectors, reflectors, triangles):
    height, width = eigenvectors.shape
    lanes = height // CHUNKS
    half = reflectors.shape[1]
    dma = pltpu.SemaphoreType.DMA
    anywhere = pl.BlockSpec(memory_space=pl.ANY)
    vmem = pl.BlockSpec(memory_space=pltpu.VMEM)
    wh, wl, vnh, vnl, xb = pl.pallas_call(
        functools.partial(gather_kernel, rows),
        out_shape=[
            pltpu.VMEM((512, width), BF16),
            pltpu.VMEM((512, width), BF16),
            pltpu.VMEM((CHUNKS, lanes, 512), BF16),
            pltpu.VMEM((CHUNKS, lanes, 512), BF16),
            pltpu.VMEM((CHUNKS, lanes, width), F32),
        ],
        in_specs=[anywhere, anywhere, vmem],
        out_specs=[vmem] * 5,
        scratch_shapes=[
            pltpu.VMEM((4, CHUNKS, 2, half, lanes), F32),
            pltpu.VMEM((CHUNKS, lanes, width), BF16),
            pltpu.VMEM((CHUNKS, lanes, width), BF16),
            pltpu.VMEM((4, 128, width), F32),
            pltpu.VMEM((512, 128), BF16),
            pltpu.VMEM((512, 128), BF16),
            pltpu.VMEM((4, 128, 128), F32),
            pltpu.VMEM((4, 16, 8, width), F32),
            pltpu.VMEM((4, 16, 8, width), F32),
            pltpu.VMEM((1, 16, 8, width), F32),
            pltpu.VMEM((48, 8, 128), F32),
            pltpu.VMEM((2, 80, 8, 128), F32),
            pltpu.VMEM((4, 4, 128, 128), F32),
            pltpu.VMEM((4, 128, 128), F32),
            pltpu.VMEM((16, 2, 8, width), F32),
            pltpu.VMEM((16, 3, 8, 128), F32),
            pltpu.VMEM((16, 1, 8, width), F32),
            pltpu.VMEM((16, 1, 8, width), F32),
            dma((CHUNKS,)), dma((CHUNKS,)), dma((CHUNKS,)), dma((CHUNKS // 2,)), dma((CHUNKS + CHUNKS // 2,)), dma, dma,
            dma((4,)), dma((4,)), dma((4,)), dma((4,)), dma((4,)), dma((4,)), pltpu.SemaphoreType.REGULAR,
        ],
        compiler_params=pltpu.CompilerParams(
            collective_id=0, has_side_effects=True, vmem_limit_bytes=36 * 2**20),
    )(reflectors.T, eigenvectors, triangles)
    return pl.pallas_call(
        update_kernel,
        out_shape=jax.ShapeDtypeStruct((height, width), F32),
        in_specs=[vmem] * 5,
        out_specs=anywhere,
        scratch_shapes=[pltpu.VMEM((CHUNKS, lanes, width), F32), dma((CHUNKS,))],
        compiler_params=pltpu.CompilerParams(vmem_limit_bytes=16 * 2**20),
    )(xb, vnh, vnl, wh, wl)


def solution(mesh):
    return jax.shard_map(
        functools.partial(on_device, mesh.shape["row"]),
        mesh=mesh,
        in_specs=(P("row", "col"), P("row", "col"), P()),
        out_specs=P("row", "col"),
        check_vma=False,
    )
```

```python
import functools

import jax
import jax.numpy as jnp
from jax import lax
from jax.experimental import pallas as pl
from jax.experimental.pallas import tpu as pltpu
from jax.sharding import PartitionSpec as P

MESH = pl.DeviceIdType.MESH
F32, BF16 = jnp.float32, jnp.bfloat16
CHUNKS = 8
SIDE = 4
OWN, UP, DOWN, FAR = range(4)
REL = (0, 1, 3, 2)
GRAM = ((OWN, UP), (UP, UP), (OWN, DOWN), (UP, DOWN), (OWN, OWN), (DOWN, DOWN),
        (UP, FAR), (FAR, FAR), (DOWN, FAR), (OWN, FAR))


def split(a):
    high = a.astype(BF16)
    return high, (a - high.astype(F32)).astype(BF16)


def dot3(a, b, dims=(((1,), (0,)), ((), ()))):
    left = jnp.concatenate([a[0], a[0], a[1]], dims[0][0][0])
    right = jnp.concatenate([b[0], b[1], b[0]], dims[0][1][0])
    return lax.dot_general(left, right, dims, preferred_element_type=F32)


NT = (((1,), (1,)), ((), ()))


def dot(a, b):
    return dot3(split(a), split(b))


def gather_kernel(rows, vt_in, x_in, t_ref, wh, wl, vnh, vnl, xb,
                  vt, xh, xl, wf, kh, kl, tb, pacc, pred, pred_l, gacc, gh, gf, mref,
                  rs_e, rs_g, rs_l, rs_o,
                  xsem, own_in, near_in, far_in_sem, z_in, sib_out, z_out, rss, rsr, ags, agr, gxs, gxr, line_in):
    me = lax.axis_index("row")
    col = lax.axis_index("col")
    z, k = lax.div(col, 2), lax.rem(col, 2)
    up = lax.rem(z + 1, 4) * 2 + k
    down = lax.rem(z + 3, 4) * 2 + k
    sib = z * 2 + 1 - k
    lanes = vt.shape[-1]

    barrier = pltpu.get_barrier_semaphore()
    for other in (up, down, sib):
        pl.semaphore_signal(barrier, inc=1, device_id=(me, other), device_id_type=MESH)
    across = [lax.rem(me + SIDE * d, rows) for d in range(1, SIDE)]
    along = [lax.div(me, SIDE) * SIDE + lax.rem(lax.rem(me, SIDE) + d, SIDE) for d in range(1, SIDE)]
    for other in across + along:
        pl.semaphore_signal(barrier, inc=1, device_id=(other, col), device_id_type=MESH)

    def own(c):
        return vt_in.at[:, pl.ds(pl.multiple_of(c * lanes, lanes), lanes)]

    def local(c):
        return pltpu.make_async_copy(own(c), vt.at[OWN, c, k], own_in.at[c])

    def load_x(c):
        return pltpu.make_async_copy(x_in.at[pl.ds(pl.multiple_of(c * lanes, lanes), lanes)], xb.at[c], xsem.at[c])

    def remote(src, dst, ssem, rsem, target):
        return pltpu.make_async_remote_copy(src_ref=src, dst_ref=dst, send_sem=ssem, recv_sem=rsem,
                                            device_id=target, device_id_type=MESH)

    def z_own(way, c):
        return remote(own(c), vt.at[(UP, DOWN)[way], c, k], z_out, z_in.at[c], (me, (down, up)[way]))

    def z_pass(way, j):
        c = (j, CHUNKS // 2 + j)[way]
        return remote(vt.at[(UP, DOWN)[way], c, k], vt.at[FAR, c, k],
                      z_out, z_in.at[CHUNKS + j], (me, (down, up)[way]))

    def to_sib(slot, c):
        src = own(c) if slot == OWN else vt.at[slot, c, k]
        arrival = own_in.at[c] if slot == OWN else far_in_sem.at[lax.rem(c, CHUNKS // 2)] if slot == FAR else near_in.at[c]
        return remote(src, vt.at[slot, c, k], sib_out, arrival, (me, sib))

    def all_of(ref, sem):
        pltpu.make_async_copy(ref, ref, sem).wait()

    def peer(d):
        return lax.rem(me + d, rows)

    def rs(kind, d):
        p = peer(d)
        src = (pacc.at[pl.ds(UP, 2), p], gacc.at[pl.ds(3 * p, 3)], pacc.at[pl.ds(FAR, 1), p], pacc.at[pl.ds(OWN, 1), p])[kind]
        dst = (rs_e, rs_g, rs_l, rs_o)[kind].at[d]
        return remote(src, dst, rss.at[kind], rsr.at[kind], (p, col))

    def piece(kind, owner):
        return (pred.at[pl.ds(UP, 2), owner], gh.at[k, pl.ds(3 * owner, 3)], pred_l.at[pl.ds(0, 1), owner],
                pred.at[pl.ds(OWN, 1), owner])[kind]

    def ag_send(kind, d):
        return remote(piece(kind, me), piece(kind, me), ags.at[kind], agr.at[kind], (peer(d), col))

    def others(kind):
        n = rows - 1
        return (rs_e, rs_g, rs_l, rs_o)[kind].at[pl.ds(1, n)]

    def far_first(fn):
        for d in sorted(range(1, rows), key=lambda d: -sum(min(i, SIDE - i) for i in divmod(d, SIDE))):
            fn(d)

    def each(fn):
        lax.fori_loop(1, rows, lambda d, _: (fn(d), 0)[1], 0)

    def reduce_scatter(kind):
        (far_first if kind == 2 else each)(lambda d: rs(kind, d).start())

    def sum_and_gather(kind):
        all_of(others(kind), rsr.at[kind])
        buf = (rs_e, rs_g, rs_l, rs_o)[kind]
        total = (pacc[UP:UP + 2, me], gacc[pl.ds(3 * me, 3)], pacc[FAR:FAR + 1, me], pacc[OWN:OWN + 1, me])[kind]
        for d in range(1, rows):
            total = total + buf[d]
        if kind == 1:
            gh[k, pl.ds(3 * me, 3)] = total
        elif kind == 0:
            pred[UP:UP + 2, me] = total
        elif kind == 2:
            pred_l[0:1, me] = total
        else:
            pred[OWN:OWN + 1, me] = total
        (far_first if kind == 2 else each)(lambda d: ag_send(kind, d).start())

    def finish_gather(kind):
        all_of(others(kind), agr.at[kind])

    def gx(i):
        half = pl.ds(0, 48)
        if i == 0:
            return remote(gh.at[k, pl.ds(0, 16)], gh.at[k, pl.ds(48, 16)], gxs.at[0], gxr.at[0], (me, down))
        if i == 1:
            return remote(gh.at[k, pl.ds(16, 16)], gh.at[k, pl.ds(64, 16)], gxs.at[1], gxr.at[1], (me, up))
        if i == 3:
            half = pl.ds(48, 32)
        return remote(gh.at[k, half], gh.at[k, half], gxs.at[i], gxr.at[i], (me, sib))

    def block(slot, c):
        return vt[slot, c].reshape(2 * vt.shape[3], lanes)

    def multiply(slot, c):
        pacc[slot] += dot3(split(block(slot, c)), (xh[c], xl[c])).reshape(16, 8, 256)

    def upright(slot, c):
        th, tl = split(block(slot, c).T)
        vnh[c, :, slot * 128:(slot + 1) * 128] = th
        vnl[c, :, slot * 128:(slot + 1) * 128] = tl

    def apply(slot, c):
        multiply(slot, c)
        upright(slot, c)

    def gram(c):
        v = [split(block(s, c)) for s in (OWN, UP, DOWN)]
        a = [split(vt[s, c, k]) for s in (OWN, UP, DOWN)]
        for i, (r, s) in enumerate(GRAM[:6]):
            gacc[8 * i:8 * i + 8] += dot3(a[r], v[s], NT).reshape(8, 8, 128)

    for c in range(CHUNKS):
        local(c).start()
        load_x(c).start()
    pl.semaphore_wait(barrier, 2 * SIDE + 1)
    for c in range(2):
        for way in range(2):
            z_own(way, c).start()
    for c in range(CHUNKS):
        to_sib(OWN, c).start()
    for other in across:
        pl.semaphore_signal(line_in, inc=1, device_id=(other, col), device_id_type=MESH)
    pacc[...] = jnp.zeros_like(pacc)
    gacc[...] = jnp.zeros_like(gacc)
    gf[...] = jnp.zeros_like(gf)
    mref[...] = jnp.zeros_like(mref)
    pred[3] = jnp.zeros_like(pred[3])
    tb[...] = jnp.zeros_like(tb)
    for slot in range(4):
        shard = lax.rem(z + REL[slot], 4)
        for i in range(4):
            tb[slot, 32 * i:32 * i + 32, 32 * i:32 * i + 32] = t_ref[4 * shard + i]

    def neighbours(c):
        all_of(vt.at[pl.ds(UP, 2), c, 1 - k], near_in.at[c])
        apply(UP, c)
        apply(DOWN, c)
        gram(c)

    def mine(c, _):
        load_x(c).wait()
        h, l = split(xb[c])
        xh[c] = h
        xl[c] = l
        all_of(vt.at[OWN, c], own_in.at[c])
        apply(OWN, c)
        return 0

    def step(c, _):
        @pl.when(c < CHUNKS // 2)
        def _():
            lax.fori_loop(2 * c, 2 * c + 2, mine, 0)

        @pl.when(c == CHUNKS // 2)
        def _():
            pl.semaphore_wait(line_in, SIDE - 1)
            reduce_scatter(3)

        @pl.when(c == CHUNKS - 2)
        def _():
            sum_and_gather(3)

        @pl.when(c > 0)
        def _():
            neighbours(c - 1)

        all_of(vt.at[pl.ds(UP, 2), c, k], z_in.at[c])

        @pl.when(c < CHUNKS - 2)
        def _():
            z_own(0, c + 2).start()
            z_own(1, c + 2).start()

        @pl.when(c >= CHUNKS - 2)
        def _():
            for i in range(2):
                j = 2 * (c - (CHUNKS - 2)) + i
                z_pass(0, j).start()
                z_pass(1, j).start()

        to_sib(UP, c).start()
        to_sib(DOWN, c).start()
        return 0

    lax.fori_loop(0, CHUNKS, step, 0)

    def far(j, *parts):
        def one(i, _):
            c = j + i * (CHUNKS // 2)
            for part in parts:
                part(c)
            return 0
        if far_in in parts:
            all_of(vt.at[FAR, pl.ds(0, 2), 1 - k], far_in_sem.at[j])
        lax.fori_loop(0, 2, one, 0)

    def far_in(c):
        multiply(FAR, c)

    def far_up(c):
        upright(FAR, c)

    def arrived(j):
        all_of(vt.at[FAR, pl.ds(0, 2), k], z_in.at[CHUNKS + j])
        to_sib(FAR, j).start()
        to_sib(FAR, CHUNKS // 2 + j).start()

    def slot_of(shard):
        rel = lax.rem(shard - z + 4, 4)
        return rel + lax.div(rel, 2) - 2 * lax.div(rel, 3)

    slots = [slot_of(s) for s in range(4)]

    def at_slot(s):
        return pl.ds(pl.multiple_of(slots[s] * 128, 128), 128)

    def assemble(first, last):
        for i in range(first, last):
            r, s = GRAM[i]
            full = gh[:, 8 * i:8 * i + 8].reshape(128, 128)
            gf[r, s] = full
            if r != s:
                gf[s, r] = full.T

    def invert(*which):
        row = lax.broadcasted_iota(jnp.int32, (128, 128), 0)
        lane = lax.broadcasted_iota(jnp.int32, (128, 128), 1)
        unit = jnp.where(lane == row, 1.0, 0.0).astype(F32)
        above = lane - lax.rem(lane, 32) > row
        n = [dot(tb[s], jnp.where(above, gf[s, s], 0.0)) for s in which]
        square = [dot(m, m) for m in n]
        both = [dot(unit - m, unit + q) for m, q in zip(n, square)]
        for s, m in zip(which, both):
            mref[s] = dot(m, tb[s])

    def substitute(rest, put):
        for s in range(3, -1, -1):
            w = dot(mref[slots[s]], rest[s])
            put(s, w)
            for r in range(s):
                rest[r] = rest[r] - dot(gf[slots[r], slots[s]], w)

    def near_w():
        def put(s, w):
            wf[slots[s]] = w
        substitute([pred[slots[s]].reshape(128, 256) for s in range(4)], put)

    def far_k():
        row = lax.broadcasted_iota(jnp.int32, (128, 128), 0)
        unit = jnp.where(lax.broadcasted_iota(jnp.int32, (128, 128), 1) == row, 1.0, 0.0).astype(F32)

        def put(s, w):
            h, l = split(w)
            kh[at_slot(s)] = h
            kl[at_slot(s)] = l
        substitute([jnp.where(slots[s] == FAR, unit, 0.0) for s in range(4)], put)

    def far_known():
        total = jnp.zeros((128, 256), F32)
        for slot in (OWN, UP, DOWN):
            after = lax.rem(z + REL[slot], 4) > lax.rem(z + 2, 4)
            total += jnp.where(after, dot(gf[FAR, slot], wf[slot]), 0.0)
        return total

    neighbours(CHUNKS - 1)
    reduce_scatter(1)
    reduce_scatter(0)
    arrived(0)
    far(0, far_in, far_up)
    sum_and_gather(1)
    arrived(1)
    far(1, far_in, far_up)
    sum_and_gather(0)
    arrived(2)
    far(2, far_in, far_up)
    arrived(3)
    far(3, far_in)
    reduce_scatter(2)
    finish_gather(1)
    for i in range(3):
        gx(i).start()
    far(3, far_up)
    gx(2).wait_recv()
    assemble(0, 6)
    invert(OWN, UP, DOWN)
    gx(0).wait_recv()
    gx(1).wait_recv()
    gx(3).start()
    sum_and_gather(2)
    finish_gather(3)
    finish_gather(0)
    near_w()
    gx(3).wait_recv()
    assemble(6, 10)
    invert(FAR)
    far_k()
    known = far_known()
    finish_gather(2)
    change = dot3((kh[...], kl[...]), split(pred_l[0].reshape(128, 256) - known))
    h, l = split(wf[...].reshape(512, 256) + jnp.where(change == change, change, 0.0))
    wh[...] = h
    wl[...] = l

    all_of(vt.at[:, :, 0], sib_out)
    all_of(vt.at[pl.ds(0, 3), :, 0], z_out)
    for i in range(4):
        gx(i).wait_send()
    for kind in range(4):
        all_of(others(kind), rss.at[kind])
        all_of(others(kind), ags.at[kind])


def update_kernel(xb, vnh, vnl, wh, wl, out, buf, sem):
    lanes = buf.shape[1]

    def store(c):
        return pltpu.make_async_copy(buf.at[c], out.at[pl.ds(pl.multiple_of(c * lanes, lanes), lanes)], sem.at[c])

    def one(c, _):
        two = pl.ds(2 * c, 2)
        left = vnh[two].reshape(2 * lanes, 512), vnl[two].reshape(2 * lanes, 512)
        buf[two] = xb[two] - dot3(left, (wh[...], wl[...])).reshape(2, lanes, 256)
        store(2 * c).start()
        store(2 * c + 1).start()
        return 0

    lax.fori_loop(0, CHUNKS // 2, one, 0)
    lax.fori_loop(0, CHUNKS, lambda c, _: (store(c).wait(), 0)[1], 0)


def on_device(rows, eigenvectors, reflectors, triangles):
    height, width = eigenvectors.shape
    lanes = height // CHUNKS
    half = reflectors.shape[1]
    dma = pltpu.SemaphoreType.DMA
    anywhere = pl.BlockSpec(memory_space=pl.ANY)
    vmem = pl.BlockSpec(memory_space=pltpu.VMEM)
    wh, wl, vnh, vnl, xb = pl.pallas_call(
        functools.partial(gather_kernel, rows),
        out_shape=[
            pltpu.VMEM((512, width), BF16),
            pltpu.VMEM((512, width), BF16),
            pltpu.VMEM((CHUNKS, lanes, 512), BF16),
            pltpu.VMEM((CHUNKS, lanes, 512), BF16),
            pltpu.VMEM((CHUNKS, lanes, width), F32),
        ],
        in_specs=[anywhere, anywhere, vmem],
        out_specs=[vmem] * 5,
        scratch_shapes=[
            pltpu.VMEM((4, CHUNKS, 2, half, lanes), F32),
            pltpu.VMEM((CHUNKS, lanes, width), BF16),
            pltpu.VMEM((CHUNKS, lanes, width), BF16),
            pltpu.VMEM((4, 128, width), F32),
            pltpu.VMEM((512, 128), BF16),
            pltpu.VMEM((512, 128), BF16),
            pltpu.VMEM((4, 128, 128), F32),
            pltpu.VMEM((4, 16, 8, width), F32),
            pltpu.VMEM((4, 16, 8, width), F32),
            pltpu.VMEM((1, 16, 8, width), F32),
            pltpu.VMEM((48, 8, 128), F32),
            pltpu.VMEM((2, 80, 8, 128), F32),
            pltpu.VMEM((4, 4, 128, 128), F32),
            pltpu.VMEM((4, 128, 128), F32),
            pltpu.VMEM((16, 2, 8, width), F32),
            pltpu.VMEM((16, 3, 8, 128), F32),
            pltpu.VMEM((16, 1, 8, width), F32),
            pltpu.VMEM((16, 1, 8, width), F32),
            dma((CHUNKS,)), dma((CHUNKS,)), dma((CHUNKS,)), dma((CHUNKS // 2,)), dma((CHUNKS + CHUNKS // 2,)), dma, dma,
            dma((4,)), dma((4,)), dma((4,)), dma((4,)), dma((4,)), dma((4,)), pltpu.SemaphoreType.REGULAR,
        ],
        compiler_params=pltpu.CompilerParams(
            collective_id=0, has_side_effects=True, vmem_limit_bytes=36 * 2**20),
    )(reflectors.T, eigenvectors, triangles)
    return pl.pallas_call(
        update_kernel,
        out_shape=jax.ShapeDtypeStruct((height, width), F32),
        in_specs=[vmem] * 5,
        out_specs=anywhere,
        scratch_shapes=[pltpu.VMEM((CHUNKS, lanes, width), F32), dma((CHUNKS,))],
        compiler_params=pltpu.CompilerParams(vmem_limit_bytes=16 * 2**20),
    )(xb, vnh, vnl, wh, wl)


def solution(mesh):
    return jax.shard_map(
        functools.partial(on_device, mesh.shape["row"]),
        mesh=mesh,
        in_specs=(P("row", "col"), P("row", "col"), P()),
        out_specs=P("row", "col"),
        check_vma=False,
    )
```
